128 devices in a mesh: space: 16 (over z, x_lo, core), chaos: 8 (over x_hi, y).
Axes of the slice: x: 4 (x_hi: 2, x_lo: 2; x = x_hi * 2 + x_lo), y: 4, z: 4, core: 2. Of those that a mesh axis runs over, the one named last changes fastest.
Arguments:
- solution: float32 [128, 32, 32, 128], P('chaos', 'space'), may hold values from -6 to 6
- mean_faces: float32 [3, 32, 32, 128], P(None, 'space'), may hold values from 0.5 to 2
- kl_faces: float32 [32, 3, 32, 32, 128], P('chaos', None, 'space'), may hold values from -3 to 3
- multi_index: int32 [128, 32], replicated, may hold values from 0 to 2, as said below
- couplings: int32 [32, 128, 2], replicated, may hold values from 0 to 128, as said below
Outputs:
- applied: float32 [128, 32, 32, 128], P('chaos', 'space')
The draws below stay inside these ranges and needn't reach their ends.
Inputs may be any that keep to these rules, and one draw needn't show every extreme that they name: `multi_index`: row 0 is the zero multi-index, rows 1 to 32 are the unit multi-indices in order, the other rows are distinct multi-indices of total degree 2 in increasing order of their two variables. couplings[k, i, 0] is the row of multi_index equal to row i plus one in variable k, couplings[k, i, 1] the row equal to row i minus one in variable k, and 128 where no such row exists.
All inputs are finite; a program needn't handle non-finite values.
Results may differ from the reference program's by a relative error of at most 0.00007.
Values sent between devices are 32-bit elements; how exact they have to be, the bound alone decides.
A program may use at most 256 MiB of HBM per device.

```python
import math
import jax
import jax.numpy as jnp
from jax import lax

P_SIZE = 128
K = 32
NX = 32
NY = 128
NZ = 32


def chaos_table(key):
    base = jax.random.fold_in(key, 11)
    codes = jnp.arange(K * K, dtype=jnp.int32)
    first = codes // K
    second = codes % K
    rank = jax.random.permutation(jax.random.fold_in(base, 1), K * K).astype(jnp.int32)
    pick = jax.random.randint(jax.random.fold_in(base, 2), (), 0, K, dtype=jnp.int32)
    score = jnp.where(first <= second, rank + 1, K * K + 1 + codes)
    score = jnp.where(codes == pick * (K + 1), 0, score)
    order = jnp.argsort(score, stable=True).astype(jnp.int32)
    chosen = jnp.sort(order[:P_SIZE - 1 - K])
    identity = jnp.eye(K, dtype=jnp.int32)
    pairs = identity[chosen // K] + identity[chosen % K]
    return jnp.concatenate([jnp.zeros((1, K), jnp.int32), identity, pairs], axis=0)


def draw_multi_index(key, part):
    return chaos_table(key)


def draw_couplings(key, part):
    table = chaos_table(key)
    identity = jnp.eye(K, dtype=jnp.int32)
    columns = jnp.arange(P_SIZE, dtype=jnp.int32)
    result = []
    for sign in (1, -1):
        target = table[None, :, :] + sign * identity[:, None, :]
        match = jnp.all(target[:, :, None, :] == table[None, None, :, :], axis=-1).astype(jnp.int32)
        found = jnp.max(match, axis=-1)
        where_row = jnp.max(match * columns[None, None, :], axis=-1)
        result.append(jnp.where(found > 0, where_row, P_SIZE).astype(jnp.int32))
    return jnp.stack(result, axis=-1)


def steps_of(key, extent, shards, least, high):
    def one(axis_at, shards_of):
        draws = jax.random.uniform(jax.random.fold_in(jax.random.fold_in(key, 6), axis_at), (shards_of,), jnp.float32, least / len(shards), high / len(shards))
        return jnp.repeat(jnp.exp(draws), extent[axis_at] // shards_of).reshape((-1,) + (1,) * (len(extent) - axis_at - 1))

    level = one(*shards[0])
    for cut in shards[1:]:
        level = level * one(*cut)
    return level


def centred(own_key, dims, scale, bound, split=(), kind=jnp.bfloat16):
    array = jax.random.normal(own_key, dims, jnp.float32) * scale
    if len(split) > 0:
        array = steps_of(own_key, dims, split, -0.22, 0.18) * array
    return jnp.clip(array, min=-bound, max=bound).astype(kind)


def setup_inputs(seed: int = 0) -> dict:
    keys = jax.random.split(jax.random.key(seed), 6)
    solution = centred(keys[0], (P_SIZE, NZ, NX, NY), 1.0, 6.0, ((0, 8), (1, 16)), jnp.float32)
    mean_faces = jnp.clip(jnp.exp(math.log(2.0) - 1.3862944 * jax.random.uniform(keys[1], (3, NZ, NX, NY), jnp.float32) ** steps_of(keys[1], (3, NZ, NX, NY), ((1, 16),), -0.2, 0.2)), 0.5, 2.0)
    kl_faces = centred(keys[2], (K, 3, NZ, NX, NY), 0.3, 3.0, ((0, 8), (2, 16)), jnp.float32)
    multi_index = draw_multi_index(jax.random.fold_in(keys[5], 71), 0)
    couplings = draw_couplings(jax.random.fold_in(keys[5], 71), 0)
    return {"solution": solution, "mean_faces": mean_faces, "kl_faces": kl_faces, "multi_index": multi_index, "couplings": couplings}


def below(face_z, plane):
    return jnp.concatenate([plane[None], face_z[:-1]], axis=0)

def operate_faces(padded, face_x, face_y, face_z, below_z):
    centre = padded[:, 1:-1]
    above = padded[:, 2:]
    beneath = padded[:, :-2]
    next_x = jnp.pad(centre[:, :, 1:], ((0, 0), (0, 0), (0, 1), (0, 0)))
    prev_x = jnp.pad(centre[:, :, :-1], ((0, 0), (0, 0), (1, 0), (0, 0)))
    next_y = jnp.pad(centre[:, :, :, 1:], ((0, 0), (0, 0), (0, 0), (0, 1)))
    prev_y = jnp.pad(centre[:, :, :, :-1], ((0, 0), (0, 0), (0, 0), (1, 0)))
    prior_x = jnp.pad(face_x[:, :-1], ((0, 0), (1, 0), (0, 0)))
    prior_y = jnp.pad(face_y[:, :, :-1], ((0, 0), (0, 0), (1, 0)))
    return face_x * (centre - next_x) + prior_x * (centre - prev_x) + face_y * (centre - next_y) + prior_y * (centre - prev_y) + face_z * (centre - above) + below_z * (centre - beneath)

def reference(solution, mean_faces, kl_faces, multi_index, couplings):
    total_modes = solution.shape[0]
    padded = jnp.pad(solution, ((0, 0), (1, 1), (0, 0), (0, 0)))
    bottom = jnp.zeros_like(mean_faces[2, 0])
    result = operate_faces(padded, mean_faces[0], mean_faces[1], mean_faces[2], below(mean_faces[2], bottom))
    degrees = multi_index.astype(jnp.float32).T
    up_rows = jnp.minimum(couplings[:, :, 0], total_modes - 1).astype(jnp.int32)
    down_rows = jnp.minimum(couplings[:, :, 1], total_modes - 1).astype(jnp.int32)
    up_weight = jnp.where(couplings[:, :, 0] < total_modes, jnp.sqrt(degrees + 1.0), 0.0)
    down_weight = jnp.where(couplings[:, :, 1] < total_modes, jnp.sqrt(degrees), 0.0)

    def add_field(index, total):
        faces = lax.dynamic_index_in_dim(kl_faces, index, 0, keepdims=False)
        upper_w = lax.dynamic_index_in_dim(up_weight, index, 0, keepdims=False)
        lower_w = lax.dynamic_index_in_dim(down_weight, index, 0, keepdims=False)
        upper_r = lax.dynamic_index_in_dim(up_rows, index, 0, keepdims=False)
        lower_r = lax.dynamic_index_in_dim(down_rows, index, 0, keepdims=False)
        mixed = upper_w[:, None, None, None] * padded[upper_r] + lower_w[:, None, None, None] * padded[lower_r]
        return total + operate_faces(mixed, faces[0], faces[1], faces[2], below(faces[2], bottom))
    return lax.fori_loop(0, K, add_field, result)
```

```python
import math

import jax
import jax.numpy as jnp
from jax import lax
from jax.experimental import pallas as pl
from jax.experimental.pallas import tpu as pltpu
from jax.sharding import PartitionSpec as P

MESH = pl.DeviceIdType.MESH
F32 = jnp.float32
I32 = jnp.int32
SLABS = 16
GROUPS = 8
MODES = 16
FIELDS = 4
KL_TILES = FIELDS * 3 + 3
UNITS = 32
FIRST_PAIR = 33
TOTAL = 128
SLOTS = 192
ROOT2 = math.sqrt(2.0)


def flip_of(slab):
    return lax.rem(lax.div(slab, 4), 2)


def block_of(slab, chaos):
    high = lax.rem(lax.div(chaos, 4) + flip_of(slab), 2)
    y = lax.rem(chaos, 4)
    return high * 4 + high * (3 - y) + (1 - high) * y


def chaos_of(slab, block):
    high = lax.div(block, 4)
    low = lax.rem(block, 4)
    y = high * (3 - low) + (1 - high) * low
    return lax.rem(high + flip_of(slab), 2) * 4 + y


def sublane():
    return lax.broadcasted_iota(I32, (8, 128), 0)


def lane():
    return lax.broadcasted_iota(I32, (8, 128), 1)


def halves(a, b):
    low = sublane() < 4
    return jnp.where(low, a, pltpu.roll(b, 4, 0)), jnp.where(low, pltpu.roll(a, 4, 0), b)


def row(ref_row):
    return jnp.broadcast_to(ref_row, (8, 128))


def make_tables(mi_ref, table_ref):
    shape = (TOTAL, TOTAL)
    mode = lax.broadcasted_iota(I32, shape, 0)
    var = lax.broadcasted_iota(I32, shape, 1)
    degree = jnp.concatenate([mi_ref[...], jnp.zeros((TOTAL - UNITS, TOTAL), I32)], axis=0).T
    is_pair = mode >= FIRST_PAIR
    held = (degree > 0) & is_pair
    count = held.astype(I32)
    running = count
    step = 1
    while step < TOTAL:
        running = running + jnp.where(mode >= step, pltpu.roll(running, step, 0), 0)
        step *= 2
    total = jnp.broadcast_to(running[TOTAL - 1 :, :], (8, TOTAL))
    var8 = lax.broadcasted_iota(I32, (8, TOTAL), 1)
    prefix = total
    step = 1
    while step < UNITS:
        prefix = prefix + jnp.where(var8 >= step, pltpu.roll(prefix, step, 1), 0)
        step *= 2
    start = prefix - total
    place = running - count + jnp.broadcast_to(start[:1, :], shape)
    first = jnp.min(jnp.where(held, var, TOTAL), axis=1, keepdims=True)
    last = jnp.max(jnp.where(held, var, -1), axis=1, keepdims=True)
    place_a = jnp.max(jnp.where(held & (var == first), place, -1), axis=1, keepdims=True)
    place_b = jnp.max(jnp.where(held & (var == last), place, -1), axis=1, keepdims=True)
    column = lax.broadcasted_iota(I32, (TOTAL, 1), 0)
    pair = column >= FIRST_PAIR
    double = first == last
    kind = jnp.where(double, 2, 1)
    first = jnp.where(pair, jnp.minimum(first, UNITS - 1), 0)
    last = jnp.where(pair, jnp.maximum(last, 0), 0)
    code_a = jnp.where(pair, ((column * UNITS + last) * UNITS + first) * 4 + kind, 0)
    code_b = jnp.where(pair & jnp.logical_not(double), ((column * UNITS + first) * UNITS + last) * 4 + kind, 0)
    code_p = (first * UNITS + last) * 4 + kind
    for half in range(2):
        slot = var + half * TOTAL
        code = jnp.where(place_a == slot, code_a, 0) + jnp.where(place_b == slot, code_b, 0)
        table_ref[half] = jnp.broadcast_to(jnp.sum(code, axis=0, keepdims=True), (8, TOTAL))
    table_ref[2] = jnp.broadcast_to(
        jnp.sum(jnp.where(mode == var, code_p, 0), axis=0, keepdims=True), (8, TOTAL)
    )
    table_ref[3] = jnp.where(total > 0, prefix - 1, -1)


def kernel(
    sol_ref, mean_ref, kl_ref, mi_ref, out_ref,
    vsol, vmean, vkl, vmi, send_v, send_k, modes, fields, zface, mean_blocks,
    halo_src_z, halo_src_x, halo_z, halo_x, diff, face, sums, result, table, table_s,
    load_sem, vs_sem, vr_sem, ks_sem, kr_sem, zs_sem, zr_sem, hs_sem, hr_sem, os_sem, or_sem, table_sem,
):
    s, c = lax.axis_index("space"), lax.axis_index("chaos")
    up, down = lax.rem(s + 1, SLABS), lax.rem(s + SLABS - 1, SLABS)
    block = block_of(s, c)
    up_c, down_c = chaos_of(up, block), chaos_of(down, block)
    next_c = chaos_of(s, lax.rem(block + 1, GROUPS))
    prev_c = chaos_of(s, lax.rem(block + GROUPS - 1, GROUPS))

    barrier = pltpu.get_barrier_semaphore()
    peers = [(s, lax.rem(c + d, GROUPS)) for d in range(1, GROUPS)]
    peers += [(up, c), (down, c), (up, up_c), (down, down_c)]
    for peer in peers:
        pl.semaphore_signal(barrier, inc=1, device_id=peer, device_id_type=MESH)

    loads = [
        pltpu.make_async_copy(src, dst, load_sem.at[i])
        for i, (src, dst) in enumerate(((sol_ref, vsol), (kl_ref, vkl), (mean_ref, vmean), (mi_ref, vmi)))
    ]
    for load in loads:
        load.start()

    loads[0].wait()

    @pl.loop(0, MODES)
    def _(i):
        for t in range(4):
            rows = pl.ds(8 * t, 8)
            low, high = halves(vsol[i, 0, rows, :], vsol[i, 1, rows, :])
            send_v[2 * t, i] = low
            send_v[2 * t + 1, i] = high

    pl.semaphore_wait(barrier, len(peers))

    loads[1].wait()
    loads[2].wait()
    z_copies = [
        pltpu.make_async_remote_copy(
            vkl.at[:, 2, 1], zface.at[pl.ds(0, FIELDS)], zs_sem.at[0], zr_sem.at[0], device_id=(up, c), device_id_type=MESH
        ),
        pltpu.make_async_remote_copy(
            vmean.at[2, 1], zface.at[FIELDS], zs_sem.at[1], zr_sem.at[1], device_id=(up, c), device_id_type=MESH
        ),
    ]
    for copy in z_copies:
        copy.start()

    def mode_copy(d):
        target = lax.rem(c + d, GROUPS)
        return pltpu.make_async_remote_copy(
            send_v.at[block_of(s, target)],
            modes.at[pl.ds(c * MODES, MODES)],
            vs_sem.at[d],
            vr_sem.at[c],
            device_id=(s, target),
            device_id_type=MESH,
        )

    for d in range(1, GROUPS):
        mode_copy(d).start()

    @pl.loop(0, MODES)
    def _(i):
        modes[c * MODES + i] = send_v[block, i]

    @pl.loop(0, FIELDS * 3)
    def _(q):
        k, dim = lax.div(q, 3), lax.rem(q, 3)
        for t in range(4):
            rows = pl.ds(8 * t, 8)
            low, high = halves(vkl[k, dim, 0, rows, :], vkl[k, dim, 1, rows, :])
            send_k[2 * t, q] = low
            send_k[2 * t + 1, q] = high

    for b in range(GROUPS):
        for k in range(FIELDS):
            for layer in range(2):
                at = pl.ds(2 * k + layer, 1)
                if b == 0:
                    send_k[b, FIELDS * 3, at, :] = jnp.zeros((1, 128), F32)
                else:
                    send_k[b, FIELDS * 3, at, :] = vkl[k, 0, layer, pl.ds(4 * b - 1, 1), :]

    for copy in z_copies:
        copy.wait()
    for pair in range(2):
        for t in range(4):
            rows = pl.ds(8 * t, 8)
            low, high = halves(zface[2 * pair, rows, :], zface[2 * pair + 1, rows, :])
            send_k[2 * t, FIELDS * 3 + 1 + pair] = low
            send_k[2 * t + 1, FIELDS * 3 + 1 + pair] = high

    def field_copy(d):
        target = lax.rem(c + d, GROUPS)
        return pltpu.make_async_remote_copy(
            send_k.at[block_of(s, target)],
            fields.at[c],
            ks_sem.at[d],
            kr_sem.at[c],
            device_id=(s, target),
            device_id_type=MESH,
        )

    for d in range(1, GROUPS):
        field_copy(d).start()

    @pl.loop(0, KL_TILES)
    def _(q):
        fields[c, q] = send_k[block, q]

    def halo_copies(group):
        cells = pl.ds(group * (MODES // 2), MODES // 2)
        targets = ((up, up_c), (down, down_c), (s, next_c), (s, prev_c))
        copies = []
        for i, target in enumerate(targets):
            source, buffer = (halo_src_z, halo_z) if i < 2 else (halo_src_x, halo_x)
            part = cells if i < 2 else group
            copies.append(
                pltpu.make_async_remote_copy(
                    source.at[i % 2, part],
                    buffer.at[i % 2, part],
                    hs_sem.at[i, group],
                    hr_sem.at[i, group],
                    device_id=target,
                    device_id_type=MESH,
                )
            )
        return copies

    def arrival(d):
        return lax.rem(c + GROUPS - d, GROUPS)

    @pl.loop(0, GROUPS)
    def _(d):
        group = arrival(d)

        @pl.when(d > 0)
        def _():
            pltpu.make_async_copy(send_v.at[0], modes.at[pl.ds(group * MODES, MODES)], vr_sem.at[group]).wait()

        @pl.loop(0, MODES // 2)
        def _(i):
            at = group * (MODES // 2) + i
            low, high = halves(modes[2 * at], modes[2 * at + 1])
            halo_src_z[0, at] = high
            halo_src_z[1, at] = low

        for half in range(2):
            for layer in range(2):
                for i in range(8):
                    m = group * MODES + half * 8 + i
                    at = pl.ds(half * 8 + i, 1)
                    halo_src_x[0, group, layer, at, :] = modes[m, pl.ds(4 * layer + 3, 1), :]
                    halo_src_x[1, group, layer, at, :] = modes[m, pl.ds(4 * layer, 1), :]
        for copy in halo_copies(group):
            copy.start()

    loads[3].wait()
    make_tables(vmi, table)
    to_scalars = pltpu.make_async_copy(table, table_s, table_sem)
    to_scalars.start()

    low4 = sublane() < 4
    sub4 = lax.rem(sublane(), 4)
    below_ok = s > 0
    for t in range(4):
        rows = pl.ds(8 * t, 8)
        parts = [halves(vmean[dim, 0, rows, :], vmean[dim, 1, rows, :]) for dim in range(3)]
        under = zface[FIELDS, rows, :]
        for h in range(2):
            b = 2 * t + h
            fx, fy, fz = (part[h] for part in parts)
            prior = pltpu.roll(fx, 1, 0)
            if b == 0:
                prior = jnp.where(sub4 == 0, 0.0, prior)
            else:
                edges = [row(vmean[0, layer, pl.ds(4 * b - 1, 1), :]) for layer in range(2)]
                prior = jnp.where(sub4 == 0, jnp.where(low4, edges[0], edges[1]), prior)
            lower = under if h == 0 else pltpu.roll(under, 4, 0)
            lower = jnp.where(below_ok, lower, 0.0)
            for q, value in enumerate((fx, prior, fy, fz, jnp.where(low4, lower, pltpu.roll(fz, 4, 0)))):
                mean_blocks[b, q] = value

    above_ok = s < SLABS - 1
    next_ok = block < GROUPS - 1
    last_lane = lane() == 127

    @pl.loop(0, GROUPS)
    def _(d):
        group = arrival(d)
        for copy in halo_copies(group):
            copy.wait_recv()

        @pl.loop(0, MODES // 2)
        def _(i):
            cell = group * (MODES // 2) + i
            under = halo_z[0, cell]
            over = jnp.where(above_ok, halo_z[1, cell], 0.0)
            for odd in range(2):
                m = 2 * cell + odd
                at = pl.ds(2 * i + odd, 1)
                v = modes[m]
                before = jnp.where(low4, row(halo_x[0, group, 0, at, :]), row(halo_x[0, group, 1, at, :]))
                after = jnp.where(low4, row(halo_x[1, group, 0, at, :]), row(halo_x[1, group, 1, at, :]))
                after = jnp.where(next_ok, after, 0.0)
                next_x = jnp.where(sub4 == 3, after, pltpu.roll(v, 7, 0))
                prev_x = jnp.where(sub4 == 0, before, pltpu.roll(v, 1, 0))
                next_y = jnp.where(last_lane, 0.0, pltpu.roll(v, 127, 1))
                swapped = pltpu.roll(v, 4, 0)
                next_z = jnp.where(low4, swapped, over if odd else pltpu.roll(over, 4, 0))
                prev_z = jnp.where(low4, pltpu.roll(under, 4, 0) if odd else under, swapped)
                for q, other in enumerate((next_x, prev_x, next_y, next_z, prev_z)):
                    diff[m, q] = v - other

    @pl.loop(0, GROUPS)
    def _(d):
        group = arrival(d)

        @pl.when(d > 0)
        def _():
            pltpu.make_async_copy(send_k.at[0], fields.at[group], kr_sem.at[group]).wait()

        for k in range(FIELDS):
            fx, fy, fz = (fields[group, 3 * k + dim] for dim in range(3))
            edges = [row(fields[group, FIELDS * 3, pl.ds(2 * k + layer, 1), :]) for layer in range(2)]
            prior = jnp.where(sub4 == 0, jnp.where(low4, edges[0], edges[1]), pltpu.roll(fx, 1, 0))
            under = fields[group, FIELDS * 3 + 1 + k // 2]
            under = under if k % 2 == 0 else pltpu.roll(under, 4, 0)
            lower = jnp.where(low4, jnp.where(below_ok, under, 0.0), pltpu.roll(fz, 4, 0))
            for q, value in enumerate((fx, prior, fy, fz, lower)):
                face[group * FIELDS + k, q] = value

    to_scalars.wait()

    first_lane = lane() == 0

    def term(k, j):
        f, g = [face[k, q] for q in range(5)], [diff[j, q] for q in range(5)]
        return (f[0] * g[0] + f[1] * g[1]) + (f[3] * g[3] + f[4] * g[4]), f[2] * g[2]

    def mean_term(m):
        f, g = [mean_blocks[block, q] for q in range(5)], [diff[m, q] for q in range(5)]
        return (f[0] * g[0] + f[1] * g[1]) + (f[3] * g[3] + f[4] * g[4]), f[2] * g[2]

    def store(m, level, flux):
        result[m] = level + flux - jnp.where(first_lane, 0.0, pltpu.roll(flux, 1, 1))

    @pl.loop(FIRST_PAIR, TOTAL, unroll=5)
    def _(p):
        code = table_s[2, 0, p]
        kind = lax.rem(code, 4)
        b = lax.rem(lax.div(code, 4), UNITS)
        a = lax.div(code, 4 * UNITS)
        weight = jnp.where(kind == 2, F32(0.5 * ROOT2), F32(1.0))
        level, flux = mean_term(p)
        level_a, flux_a = term(a, 1 + b)
        level_b, flux_b = term(b, 1 + a)
        store(p, level + weight * (level_a + level_b), flux + weight * (flux_a + flux_b))

    zero = jnp.zeros((8, 128), F32)

    @pl.loop(0, SLOTS, init_carry=(I32(-1), zero, zero), unroll=4)
    def _(t, carry):
        before, level, flux = carry
        code = table_s[lax.div(t, TOTAL), 0, lax.rem(t, TOTAL)]
        kind = lax.rem(code, 4)
        unit = lax.rem(lax.div(code, 4), UNITS)
        k = lax.rem(lax.div(code, 4 * UNITS), UNITS)
        p = lax.div(code, 4 * UNITS * UNITS)
        weight = jnp.where(kind == 2, F32(ROOT2), jnp.where(kind == 1, F32(1.0), F32(0.0)))
        keep = jnp.where(unit == before, F32(1.0), F32(0.0))
        level_t, flux_t = term(k, p)
        level = keep * level + weight * level_t
        flux = keep * flux + weight * flux_t
        sums[t, 0] = level
        sums[t, 1] = flux
        return unit, level, flux

    @pl.loop(0, UNITS, unroll=4)
    def _(i):
        end = table_s[3, 0, i]
        weight = jnp.where(end >= 0, F32(1.0), F32(0.0))
        end = jnp.maximum(end, 0)
        level, flux = mean_term(1 + i)
        level_0, flux_0 = term(i, 0)
        store(1 + i, level + level_0 + weight * sums[end, 0], flux + flux_0 + weight * sums[end, 1])

    @pl.loop(0, UNITS, init_carry=mean_term(0), unroll=4)
    def total(k, carry):
        level, flux = term(k, 1 + k)
        return carry[0] + level, carry[1] + flux

    store(0, *total)

    def result_copy(d):
        target = lax.rem(c + d, GROUPS)
        return pltpu.make_async_remote_copy(
            result.at[pl.ds(target * MODES, MODES)],
            out_ref.at[block],
            os_sem.at[d],
            or_sem.at[block],
            device_id=(s, target),
            device_id_type=MESH,
        )

    for d in range(1, GROUPS):
        result_copy(d).start()
    own = pltpu.make_async_copy(result.at[pl.ds(c * MODES, MODES)], out_ref.at[block], or_sem.at[block])
    own.start()
    own.wait()
    for d in range(1, GROUPS):
        theirs = block_of(s, arrival(d))
        pltpu.make_async_copy(result.at[pl.ds(0, MODES)], out_ref.at[theirs], or_sem.at[theirs]).wait()
    for d in range(1, GROUPS):
        mode_copy(d).wait_send()
        field_copy(d).wait_send()
        result_copy(d).wait_send()

    @pl.loop(0, GROUPS)
    def _(d):
        for copy in halo_copies(arrival(d)):
            copy.wait_send()


def unpack(blocks_ref, out_ref):
    @pl.loop(0, MODES)
    def _(i):
        for t in range(4):
            rows = pl.ds(8 * t, 8)
            low, high = halves(blocks_ref[2 * t, i], blocks_ref[2 * t + 1, i])
            out_ref[i, 0, rows, :] = low
            out_ref[i, 1, rows, :] = high


def shards(sol, mean, kl, multi_index, couplings):
    tile = (8, 128)
    sem = pltpu.SemaphoreType.DMA
    blocks = pl.pallas_call(
        kernel,
        out_shape=jax.ShapeDtypeStruct((GROUPS, MODES) + tile, F32),
        in_specs=[pl.BlockSpec(memory_space=pltpu.HBM)] * 4,
        out_specs=pl.BlockSpec(memory_space=pl.ANY),
        scratch_shapes=[
            pltpu.VMEM((MODES, 2, 32, 128), F32),
            pltpu.VMEM((3, 2, 32, 128), F32),
            pltpu.VMEM((FIELDS, 3, 2, 32, 128), F32),
            pltpu.VMEM((UNITS, TOTAL), I32),
            pltpu.VMEM((GROUPS, MODES) + tile, F32),
            pltpu.VMEM((GROUPS, KL_TILES) + tile, F32),
            pltpu.VMEM((TOTAL,) + tile, F32),
            pltpu.VMEM((GROUPS, KL_TILES) + tile, F32),
            pltpu.VMEM((FIELDS + 1, 32, 128), F32),
            pltpu.VMEM((GROUPS, 5) + tile, F32),
            pltpu.VMEM((2, TOTAL // 2) + tile, F32),
            pltpu.VMEM((2, GROUPS, 2, MODES, 128), F32),
            pltpu.VMEM((2, TOTAL // 2) + tile, F32),
            pltpu.VMEM((2, GROUPS, 2, MODES, 128), F32),
            pltpu.VMEM((TOTAL, 5) + tile, F32),
            pltpu.VMEM((UNITS, 5) + tile, F32),
            pltpu.VMEM((SLOTS, 2) + tile, F32),
            pltpu.VMEM((TOTAL,) + tile, F32),
            pltpu.VMEM((4,) + tile, I32),
            pltpu.SMEM((4,) + tile, I32),
            sem((4,)),
            sem((GROUPS,)),
            sem((GROUPS,)),
            sem((GROUPS,)),
            sem((GROUPS,)),
            sem((2,)),
            sem((2,)),
            sem((4, GROUPS)),
            sem((4, GROUPS)),
            sem((GROUPS,)),
            sem((GROUPS,)),
            sem,
        ],
        compiler_params=pltpu.CompilerParams(
            collective_id=0, has_side_effects=True, vmem_limit_bytes=60 * 2**20
        ),
        name="apply",
    )(sol, mean, kl, multi_index.T)
    return pl.pallas_call(
        unpack,
        out_shape=jax.ShapeDtypeStruct((MODES, 2, 32, 128), F32),
        in_specs=[pl.BlockSpec(memory_space=pltpu.VMEM)],
        out_specs=pl.BlockSpec(memory_space=pltpu.VMEM),
        name="unpack",
    )(blocks)


def solution(mesh):
    return jax.shard_map(
        shards,
        mesh=mesh,
        in_specs=(
            P("chaos", "space", None, None),
            P(None, "space", None, None),
            P("chaos", None, "space", None, None),
            P(),
            P(),
        ),
        out_specs=P("chaos", "space", None, None),
        check_vma=False,
    )
```

```python
import math

import jax
import jax.numpy as jnp
from jax import lax
from jax.experimental import pallas as pl
from jax.experimental.pallas import tpu as pltpu
from jax.sharding import PartitionSpec as P

MESH = pl.DeviceIdType.MESH
F32 = jnp.float32
I32 = jnp.int32
SLABS = 16
GROUPS = 8
MODES = 16
FIELDS = 4
KL_TILES = FIELDS * 3 + 3
UNITS = 32
FIRST_PAIR = 33
TOTAL = 128
SLOTS = 192
PAIR_UNROLL = 19
SLOT_UNROLL = 16
UNIT_UNROLL = 8
ROOT2 = math.sqrt(2.0)


def flip_of(slab):
    return lax.rem(lax.div(slab, 4), 2)


def block_of(slab, chaos):
    high = lax.rem(lax.div(chaos, 4) + flip_of(slab), 2)
    y = lax.rem(chaos, 4)
    return high * 4 + high * (3 - y) + (1 - high) * y


def chaos_of(slab, block):
    high = lax.div(block, 4)
    low = lax.rem(block, 4)
    y = high * (3 - low) + (1 - high) * low
    return lax.rem(high + flip_of(slab), 2) * 4 + y


def sublane():
    return lax.broadcasted_iota(I32, (8, 128), 0)


def lane():
    return lax.broadcasted_iota(I32, (8, 128), 1)


def halves(a, b):
    low = sublane() < 4
    return jnp.where(low, a, pltpu.roll(b, 4, 0)), jnp.where(low, pltpu.roll(a, 4, 0), b)


def row(ref_row):
    return jnp.broadcast_to(ref_row, (8, 128))


def make_tables(mi_ref, table_ref):
    shape = (TOTAL, TOTAL)
    mode = lax.broadcasted_iota(I32, shape, 0)
    var = lax.broadcasted_iota(I32, shape, 1)
    degree = jnp.concatenate([mi_ref[...], jnp.zeros((TOTAL - UNITS, TOTAL), I32)], axis=0).T
    is_pair = mode >= FIRST_PAIR
    held = (degree > 0) & is_pair
    count = held.astype(I32)
    running = count
    step = 1
    while step < TOTAL:
        running = running + jnp.where(mode >= step, pltpu.roll(running, step, 0), 0)
        step *= 2
    total = jnp.broadcast_to(running[TOTAL - 1 :, :], (8, TOTAL))
    var8 = lax.broadcasted_iota(I32, (8, TOTAL), 1)
    prefix = total
    step = 1
    while step < UNITS:
        prefix = prefix + jnp.where(var8 >= step, pltpu.roll(prefix, step, 1), 0)
        step *= 2
    start = prefix - total
    place = running - count + jnp.broadcast_to(start[:1, :], shape)
    first = jnp.min(jnp.where(held, var, TOTAL), axis=1, keepdims=True)
    last = jnp.max(jnp.where(held, var, -1), axis=1, keepdims=True)
    place_a = jnp.max(jnp.where(held & (var == first), place, -1), axis=1, keepdims=True)
    place_b = jnp.max(jnp.where(held & (var == last), place, -1), axis=1, keepdims=True)
    column = lax.broadcasted_iota(I32, (TOTAL, 1), 0)
    pair = column >= FIRST_PAIR
    double = first == last
    kind = jnp.where(double, 2, 1)
    first = jnp.where(pair, jnp.minimum(first, UNITS - 1), 0)
    last = jnp.where(pair, jnp.maximum(last, 0), 0)
    code_a = jnp.where(pair, (column - FIRST_PAIR) * 2 * UNITS + first, 0)
    code_b = jnp.where(pair & jnp.logical_not(double), ((column - FIRST_PAIR) * 2 + 1) * UNITS + last, 0)
    code_p = (first * UNITS + last) * 4 + kind
    for half in range(2):
        slot = var + half * TOTAL
        code = jnp.where(place_a == slot, code_a, 0) + jnp.where(place_b == slot, code_b, 0)
        table_ref[half] = jnp.broadcast_to(jnp.sum(code, axis=0, keepdims=True), (8, TOTAL))
    table_ref[2] = jnp.broadcast_to(
        jnp.sum(jnp.where(mode == var, code_p, 0), axis=0, keepdims=True), (8, TOTAL)
    )
    table_ref[3] = jnp.where(total > 0, prefix - 1, -1)


def kernel(
    sol_ref, mean_ref, kl_ref, mi_ref, out_ref,
    vsol, vmean, vkl, vmi, send_v, send_k, modes, fields, zface, mean_blocks,
    halo_src_z, halo_src_x, halo_z, halo_x, diff, face, images, sums, result, table, table_s,
    load_sem, vs_sem, vr_sem, ks_sem, kr_sem, zs_sem, zr_sem, hs_sem, hr_sem, os_sem, or_sem, table_sem,
):
    s, c = lax.axis_index("space"), lax.axis_index("chaos")
    up, down = lax.rem(s + 1, SLABS), lax.rem(s + SLABS - 1, SLABS)
    block = block_of(s, c)
    up_c, down_c = chaos_of(up, block), chaos_of(down, block)
    next_c = chaos_of(s, lax.rem(block + 1, GROUPS))
    prev_c = chaos_of(s, lax.rem(block + GROUPS - 1, GROUPS))

    barrier = pltpu.get_barrier_semaphore()
    peers = [(s, lax.rem(c + d, GROUPS)) for d in range(1, GROUPS)]
    peers += [(up, c), (down, c), (up, up_c), (down, down_c)]
    for peer in peers:
        pl.semaphore_signal(barrier, inc=1, device_id=peer, device_id_type=MESH)

    loads = [
        pltpu.make_async_copy(src, dst, load_sem.at[i])
        for i, (src, dst) in enumerate(((sol_ref, vsol), (kl_ref, vkl), (mean_ref, vmean), (mi_ref, vmi)))
    ]
    for load in loads:
        load.start()

    loads[0].wait()

    @pl.loop(0, MODES, unroll=4)
    def _(i):
        for t in range(4):
            rows = pl.ds(8 * t, 8)
            low, high = halves(vsol[i, 0, rows, :], vsol[i, 1, rows, :])
            send_v[2 * t, i] = low
            send_v[2 * t + 1, i] = high

    pl.semaphore_wait(barrier, len(peers))

    loads[1].wait()
    loads[2].wait()
    z_copies = [
        pltpu.make_async_remote_copy(
            vkl.at[:, 2, 1], zface.at[pl.ds(0, FIELDS)], zs_sem.at[0], zr_sem.at[0], device_id=(up, c), device_id_type=MESH
        ),
        pltpu.make_async_remote_copy(
            vmean.at[2, 1], zface.at[FIELDS], zs_sem.at[1], zr_sem.at[1], device_id=(up, c), device_id_type=MESH
        ),
    ]
    for copy in z_copies:
        copy.start()

    def mode_copy(d):
        target = lax.rem(c + d, GROUPS)
        return pltpu.make_async_remote_copy(
            send_v.at[block_of(s, target)],
            modes.at[pl.ds(c * MODES, MODES)],
            vs_sem.at[d],
            vr_sem.at[c],
            device_id=(s, target),
            device_id_type=MESH,
        )

    for d in range(1, GROUPS):
        mode_copy(d).start()

    @pl.loop(0, MODES, unroll=True)
    def _(i):
        modes[c * MODES + i] = send_v[block, i]

    @pl.loop(0, FIELDS * 3, unroll=4)
    def _(q):
        k, dim = lax.div(q, 3), lax.rem(q, 3)
        for t in range(4):
            rows = pl.ds(8 * t, 8)
            low, high = halves(vkl[k, dim, 0, rows, :], vkl[k, dim, 1, rows, :])
            send_k[2 * t, q] = low
            send_k[2 * t + 1, q] = high

    for b in range(GROUPS):
        for k in range(FIELDS):
            for layer in range(2):
                at = pl.ds(2 * k + layer, 1)
                if b == 0:
                    send_k[b, FIELDS * 3, at, :] = jnp.zeros((1, 128), F32)
                else:
                    send_k[b, FIELDS * 3, at, :] = vkl[k, 0, layer, pl.ds(4 * b - 1, 1), :]

    for copy in z_copies:
        copy.wait()
    for pair in range(2):
        for t in range(4):
            rows = pl.ds(8 * t, 8)
            low, high = halves(zface[2 * pair, rows, :], zface[2 * pair + 1, rows, :])
            send_k[2 * t, FIELDS * 3 + 1 + pair] = low
            send_k[2 * t + 1, FIELDS * 3 + 1 + pair] = high

    def field_copy(d):
        target = lax.rem(c + d, GROUPS)
        return pltpu.make_async_remote_copy(
            send_k.at[block_of(s, target)],
            fields.at[c],
            ks_sem.at[d],
            kr_sem.at[c],
            device_id=(s, target),
            device_id_type=MESH,
        )

    for d in range(1, GROUPS):
        field_copy(d).start()

    @pl.loop(0, KL_TILES, unroll=True)
    def _(q):
        fields[c, q] = send_k[block, q]

    def halo_copies(group):
        cells = pl.ds(group * (MODES // 2), MODES // 2)
        targets = ((up, up_c), (down, down_c), (s, next_c), (s, prev_c))
        copies = []
        for i, target in enumerate(targets):
            source, buffer = (halo_src_z, halo_z) if i < 2 else (halo_src_x, halo_x)
            part = cells if i < 2 else group
            copies.append(
                pltpu.make_async_remote_copy(
                    source.at[i % 2, part],
                    buffer.at[i % 2, part],
                    hs_sem.at[i, group],
                    hr_sem.at[i, group],
                    device_id=target,
                    device_id_type=MESH,
                )
            )
        return copies

    def arrival(d):
        return lax.rem(c + GROUPS - d, GROUPS)

    @pl.loop(0, GROUPS)
    def _(d):
        group = arrival(d)

        @pl.when(d > 0)
        def _():
            pltpu.make_async_copy(send_v.at[0], modes.at[pl.ds(group * MODES, MODES)], vr_sem.at[group]).wait()

        @pl.loop(0, MODES // 2, unroll=True)
        def _(i):
            at = group * (MODES // 2) + i
            low, high = halves(modes[2 * at], modes[2 * at + 1])
            halo_src_z[0, at] = high
            halo_src_z[1, at] = low

        for half in range(2):
            for layer in range(2):
                for i in range(8):
                    m = group * MODES + half * 8 + i
                    at = pl.ds(half * 8 + i, 1)
                    halo_src_x[0, group, layer, at, :] = modes[m, pl.ds(4 * layer + 3, 1), :]
                    halo_src_x[1, group, layer, at, :] = modes[m, pl.ds(4 * layer, 1), :]
        for copy in halo_copies(group):
            copy.start()

    loads[3].wait()
    make_tables(vmi, table)
    to_scalars = pltpu.make_async_copy(table, table_s, table_sem)
    to_scalars.start()

    low4 = sublane() < 4
    sub4 = lax.rem(sublane(), 4)
    below_ok = s > 0
    for t in range(4):
        rows = pl.ds(8 * t, 8)
        parts = [halves(vmean[dim, 0, rows, :], vmean[dim, 1, rows, :]) for dim in range(3)]
        under = zface[FIELDS, rows, :]
        for h in range(2):
            b = 2 * t + h
            fx, fy, fz = (part[h] for part in parts)
            prior = pltpu.roll(fx, 1, 0)
            if b == 0:
                prior = jnp.where(sub4 == 0, 0.0, prior)
            else:
                edges = [row(vmean[0, layer, pl.ds(4 * b - 1, 1), :]) for layer in range(2)]
                prior = jnp.where(sub4 == 0, jnp.where(low4, edges[0], edges[1]), prior)
            lower = under if h == 0 else pltpu.roll(under, 4, 0)
            lower = jnp.where(below_ok, lower, 0.0)
            for q, value in enumerate((fx, prior, fy, fz, jnp.where(low4, lower, pltpu.roll(fz, 4, 0)))):
                mean_blocks[b, q] = value

    above_ok = s < SLABS - 1
    next_ok = block < GROUPS - 1
    last_lane = lane() == 127

    @pl.loop(0, GROUPS)
    def _(d):
        group = arrival(d)
        for copy in halo_copies(group):
            copy.wait_recv()

        @pl.loop(0, MODES // 2, unroll=True)
        def _(i):
            cell = group * (MODES // 2) + i
            under = halo_z[0, cell]
            over = jnp.where(above_ok, halo_z[1, cell], 0.0)
            for odd in range(2):
                m = 2 * cell + odd
                at = pl.ds(2 * i + odd, 1)
                v = modes[m]
                before = jnp.where(low4, row(halo_x[0, group, 0, at, :]), row(halo_x[0, group, 1, at, :]))
                after = jnp.where(low4, row(halo_x[1, group, 0, at, :]), row(halo_x[1, group, 1, at, :]))
                after = jnp.where(next_ok, after, 0.0)
                next_x = jnp.where(sub4 == 3, after, pltpu.roll(v, 7, 0))
                prev_x = jnp.where(sub4 == 0, before, pltpu.roll(v, 1, 0))
                next_y = jnp.where(last_lane, 0.0, pltpu.roll(v, 127, 1))
                swapped = pltpu.roll(v, 4, 0)
                next_z = jnp.where(low4, swapped, over if odd else pltpu.roll(over, 4, 0))
                prev_z = jnp.where(low4, pltpu.roll(under, 4, 0) if odd else under, swapped)
                for q, other in enumerate((next_x, prev_x, next_y, next_z, prev_z)):
                    diff[m, q] = v - other

    @pl.loop(0, GROUPS)
    def _(d):
        group = arrival(d)

        @pl.when(d > 0)
        def _():
            pltpu.make_async_copy(send_k.at[0], fields.at[group], kr_sem.at[group]).wait()

        for k in range(FIELDS):
            fx, fy, fz = (fields[group, 3 * k + dim] for dim in range(3))
            edges = [row(fields[group, FIELDS * 3, pl.ds(2 * k + layer, 1), :]) for layer in range(2)]
            prior = jnp.where(sub4 == 0, jnp.where(low4, edges[0], edges[1]), pltpu.roll(fx, 1, 0))
            under = fields[group, FIELDS * 3 + 1 + k // 2]
            under = under if k % 2 == 0 else pltpu.roll(under, 4, 0)
            lower = jnp.where(low4, jnp.where(below_ok, under, 0.0), pltpu.roll(fz, 4, 0))
            for q, value in enumerate((fx, prior, fy, fz, lower)):
                face[group * FIELDS + k, q] = value

    to_scalars.wait()

    first_lane = lane() == 0
    mean = [mean_blocks[block, q] for q in range(5)]

    def planes(ref, at):
        return [ref[at, q] for q in range(5)]

    def term(f, g):
        return (f[0] * g[0] + f[1] * g[1]) + (f[3] * g[3] + f[4] * g[4]), f[2] * g[2]

    def gather(level, flux):
        return level + (flux - jnp.where(first_lane, 0.0, pltpu.roll(flux, 1, 1)))

    @pl.loop(FIRST_PAIR, TOTAL, unroll=PAIR_UNROLL)
    def _(p):
        code = table_s[2, 0, p]
        kind = code & 3
        b = (code >> 2) & (UNITS - 1)
        a = code >> 7
        double = kind == 2
        weight = jnp.where(double, F32(0.5 * ROOT2), F32(1.0))
        raised = jnp.where(double, F32(ROOT2), F32(1.0))
        face_a, face_b, own = planes(face, a), planes(face, b), planes(diff, p)
        level, flux = term(mean, own)
        level_a, flux_a = term(face_a, planes(diff, 1 + b))
        level_b, flux_b = term(face_b, planes(diff, 1 + a))
        result[p] = gather(level + weight * (level_a + level_b), flux + weight * (flux_a + flux_b))
        at = 2 * (p - FIRST_PAIR)
        images[at] = raised * gather(*term(face_b, own))
        images[at + 1] = raised * gather(*term(face_a, own))

    zero = jnp.zeros((8, 128), F32)

    @pl.loop(0, SLOTS, init_carry=(I32(-1), zero), unroll=SLOT_UNROLL)
    def _(t, carry):
        before, held = carry
        code = table_s[t >> 7, 0, t & (TOTAL - 1)]
        unit = code & (UNITS - 1)
        held = jnp.where(unit == before, held, 0.0) + images[code >> 5]
        sums[t] = held
        return unit, held

    zeroth = planes(diff, 0)

    @pl.loop(0, UNITS, init_carry=term(mean, zeroth), unroll=UNIT_UNROLL)
    def total(i, carry):
        end = table_s[3, 0, i]
        weight = jnp.where(end >= 0, F32(1.0), F32(0.0))
        field, own = planes(face, i), planes(diff, 1 + i)
        level, flux = term(mean, own)
        level_0, flux_0 = term(field, zeroth)
        result[1 + i] = gather(level + level_0, flux + flux_0) + weight * sums[jnp.maximum(end, 0)]
        level_1, flux_1 = term(field, own)
        return carry[0] + level_1, carry[1] + flux_1

    result[0] = gather(*total)

    def result_copy(d):
        target = lax.rem(c + d, GROUPS)
        return pltpu.make_async_remote_copy(
            result.at[pl.ds(target * MODES, MODES)],
            out_ref.at[block],
            os_sem.at[d],
            or_sem.at[block],
            device_id=(s, target),
            device_id_type=MESH,
        )

    for d in range(1, GROUPS):
        result_copy(d).start()
    own = pltpu.make_async_copy(result.at[pl.ds(c * MODES, MODES)], out_ref.at[block], or_sem.at[block])
    own.start()
    own.wait()
    for d in range(1, GROUPS):
        theirs = block_of(s, arrival(d))
        pltpu.make_async_copy(result.at[pl.ds(0, MODES)], out_ref.at[theirs], or_sem.at[theirs]).wait()
    for d in range(1, GROUPS):
        mode_copy(d).wait_send()
        field_copy(d).wait_send()
        result_copy(d).wait_send()

    @pl.loop(0, GROUPS)
    def _(d):
        for copy in halo_copies(arrival(d)):
            copy.wait_send()


def unpack(blocks_ref, out_ref):
    @pl.loop(0, MODES)
    def _(i):
        for t in range(4):
            rows = pl.ds(8 * t, 8)
            low, high = halves(blocks_ref[2 * t, i], blocks_ref[2 * t + 1, i])
            out_ref[i, 0, rows, :] = low
            out_ref[i, 1, rows, :] = high


def shards(sol, mean, kl, multi_index, couplings):
    tile = (8, 128)
    sem = pltpu.SemaphoreType.DMA
    blocks = pl.pallas_call(
        kernel,
        out_shape=jax.ShapeDtypeStruct((GROUPS, MODES) + tile, F32),
        in_specs=[pl.BlockSpec(memory_space=pltpu.HBM)] * 4,
        out_specs=pl.BlockSpec(memory_space=pl.ANY),
        scratch_shapes=[
            pltpu.VMEM((MODES, 2, 32, 128), F32),
            pltpu.VMEM((3, 2, 32, 128), F32),
            pltpu.VMEM((FIELDS, 3, 2, 32, 128), F32),
            pltpu.VMEM((UNITS, TOTAL), I32),
            pltpu.VMEM((GROUPS, MODES) + tile, F32),
            pltpu.VMEM((GROUPS, KL_TILES) + tile, F32),
            pltpu.VMEM((TOTAL,) + tile, F32),
            pltpu.VMEM((GROUPS, KL_TILES) + tile, F32),
            pltpu.VMEM((FIELDS + 1, 32, 128), F32),
            pltpu.VMEM((GROUPS, 5) + tile, F32),
            pltpu.VMEM((2, TOTAL // 2) + tile, F32),
            pltpu.VMEM((2, GROUPS, 2, MODES, 128), F32),
            pltpu.VMEM((2, TOTAL // 2) + tile, F32),
            pltpu.VMEM((2, GROUPS, 2, MODES, 128), F32),
            pltpu.VMEM((TOTAL, 5) + tile, F32),
            pltpu.VMEM((UNITS, 5) + tile, F32),
            pltpu.VMEM((SLOTS,) + tile, F32),
            pltpu.VMEM((SLOTS,) + tile, F32),
            pltpu.VMEM((TOTAL,) + tile, F32),
            pltpu.VMEM((4,) + tile, I32),
            pltpu.SMEM((4,) + tile, I32),
            sem((4,)),
            sem((GROUPS,)),
            sem((GROUPS,)),
            sem((GROUPS,)),
            sem((GROUPS,)),
            sem((2,)),
            sem((2,)),
            sem((4, GROUPS)),
            sem((4, GROUPS)),
            sem((GROUPS,)),
            sem((GROUPS,)),
            sem,
        ],
        compiler_params=pltpu.CompilerParams(
            collective_id=0, has_side_effects=True, vmem_limit_bytes=60 * 2**20
        ),
        name="apply",
    )(sol, mean, kl, multi_index.T)
    return pl.pallas_call(
        unpack,
        out_shape=jax.ShapeDtypeStruct((MODES, 2, 32, 128), F32),
        in_specs=[pl.BlockSpec(memory_space=pltpu.VMEM)],
        out_specs=pl.BlockSpec(memory_space=pltpu.VMEM),
        name="unpack",
    )(blocks)


def solution(mesh):
    return jax.shard_map(
        shards,
        mesh=mesh,
        in_specs=(
            P("chaos", "space", None, None),
            P(None, "space", None, None),
            P("chaos", None, "space", None, None),
            P(),
            P(),
        ),
        out_specs=P("chaos", "space", None, None),
        check_vma=False,
    )
```

```python
import math

import jax
import jax.numpy as jnp
from jax import lax
from jax.experimental import pallas as pl
from jax.experimental.pallas import tpu as pltpu
from jax.sharding import PartitionSpec as P

MESH = pl.DeviceIdType.MESH
F32 = jnp.float32
I32 = jnp.int32
SLABS = 16
GROUPS = 8
MODES = 16
FIELDS = 4
KL_TILES = FIELDS * 3 + 3
UNITS = 32
FIRST_PAIR = 33
TOTAL = 128
SLOTS = 192
FULL_GROUP = 3
IMAGE_UNROLL = 95
SLOT_UNROLL = 48
RUNS = 4
UNIT_UNROLL = 32
ROOT2 = math.sqrt(2.0)


def flip_of(slab):
    return lax.rem(lax.div(slab, 4), 2)


def block_of(slab, chaos):
    high = lax.rem(lax.div(chaos, 4) + flip_of(slab), 2)
    y = lax.rem(chaos, 4)
    return high * 4 + high * (3 - y) + (1 - high) * y


def chaos_of(slab, block):
    high = lax.div(block, 4)
    low = lax.rem(block, 4)
    y = high * (3 - low) + (1 - high) * low
    return lax.rem(high + flip_of(slab), 2) * 4 + y


def peer_of(chaos, d):
    high = lax.rem(lax.div(chaos, 4) + lax.div(d, 4), 2)
    return high * 4 + lax.rem(lax.rem(chaos, 4) + lax.rem(d, 4), 4)


def source_of(chaos, d):
    high = lax.rem(lax.div(chaos, 4) + lax.div(d, 4), 2)
    return high * 4 + lax.rem(lax.rem(chaos, 4) + 4 - lax.rem(d, 4), 4)


def out_peer(chaos, d):
    d = lax.rem(d, 8)
    move = d * 0
    move = move + jnp.where(d == 1, 6, 0)
    move = move + jnp.where(d == 2, 2, 0)
    move = move + jnp.where(d == 3, 5, 0)
    move = move + jnp.where(d == 4, 7, 0)
    move = move + jnp.where(d == 5, 4, 0)
    move = move + jnp.where(d == 6, 1, 0)
    move = move + jnp.where(d == 7, 3, 0)
    high = lax.rem(lax.div(chaos, 4) + lax.div(move, 4), 2)
    return high * 4 + lax.rem(lax.rem(chaos, 4) + lax.rem(move, 4), 4)


def sublane():
    return lax.broadcasted_iota(I32, (8, 128), 0)


def lane():
    return lax.broadcasted_iota(I32, (8, 128), 1)


def halves(a, b):
    low = sublane() < 4
    return jnp.where(low, a, pltpu.roll(b, 4, 0)), jnp.where(low, pltpu.roll(a, 4, 0), b)


def row(ref_row):
    return jnp.broadcast_to(ref_row, (8, 128))


def make_tables(mi_ref, table_ref):
    shape = (TOTAL, TOTAL)
    mode = lax.broadcasted_iota(I32, shape, 0)
    var = lax.broadcasted_iota(I32, shape, 1)
    degree = jnp.concatenate([mi_ref[...], jnp.zeros((TOTAL - UNITS, TOTAL), I32)], axis=0).T
    is_pair = mode >= FIRST_PAIR
    held = (degree > 0) & is_pair
    count = held.astype(I32)
    running = count
    step = 1
    while step < TOTAL:
        running = running + jnp.where(mode >= step, pltpu.roll(running, step, 0), 0)
        step *= 2
    total = jnp.broadcast_to(running[TOTAL - 1 :, :], (8, TOTAL))
    var8 = lax.broadcasted_iota(I32, (8, TOTAL), 1)
    prefix = total
    step = 1
    while step < UNITS:
        prefix = prefix + jnp.where(var8 >= step, pltpu.roll(prefix, step, 1), 0)
        step *= 2
    start = prefix - total
    place = running - count + jnp.broadcast_to(start[:1, :], shape)
    first = jnp.min(jnp.where(held, var, TOTAL), axis=1, keepdims=True)
    last = jnp.max(jnp.where(held, var, -1), axis=1, keepdims=True)
    place_a = jnp.max(jnp.where(held & (var == first), place, -1), axis=1, keepdims=True)
    place_b = jnp.max(jnp.where(held & (var == last), place, -1), axis=1, keepdims=True)
    column = lax.broadcasted_iota(I32, (TOTAL, 1), 0)
    pair = column >= FIRST_PAIR
    double = first == last
    kind = jnp.where(double, 2, 1)
    first = jnp.where(pair, jnp.minimum(first, UNITS - 1), 0)
    last = jnp.where(pair, jnp.maximum(last, 0), 0)
    code_a = jnp.where(pair, (column - FIRST_PAIR) * 2 * UNITS + first, 0)
    code_b = jnp.where(pair & jnp.logical_not(double), ((column - FIRST_PAIR) * 2 + 1) * UNITS + last, 0)
    code_p = (first * UNITS + last) * 4 + kind
    for half in range(2):
        slot = var + half * TOTAL
        code = jnp.where(place_a == slot, code_a, 0) + jnp.where(place_b == slot, code_b, 0)
        table_ref[half] = jnp.broadcast_to(jnp.sum(code, axis=0, keepdims=True), (8, TOTAL))
    table_ref[2] = jnp.broadcast_to(
        jnp.sum(jnp.where(mode == var, code_p, 0), axis=0, keepdims=True), (8, TOTAL)
    )
    end = prefix - 1
    run = SLOTS // RUNS
    first_run = sum((start >= r * run).astype(I32) for r in range(1, RUNS))
    last_run = sum((end >= r * run).astype(I32) for r in range(1, RUNS))
    table_ref[3] = jnp.where(total > 0, end, SLOTS)
    table_ref[4] = jnp.where((total > 0) & (last_run > first_run), last_run * run - 1, SLOTS)


def kernel(
    sol_ref, mean_ref, kl_ref, mi_ref, out_ref,
    vsol, vmean, vkl, vmi, send_v, send_k, modes, fields, zface, mean_blocks,
    halo_src_z, halo_src_x, halo_z, halo_x, diff, face, images, sums, result, table, table_s,
    load_sem, vs_sem, vr_sem, ks_sem, kr_sem, zs_sem, zr_sem, hs_sem, hr_sem, os_sem, or_sem, table_sem,
):
    s, c = lax.axis_index("space"), lax.axis_index("chaos")
    up, down = lax.rem(s + 1, SLABS), lax.rem(s + SLABS - 1, SLABS)
    block = block_of(s, c)
    up_c, down_c = chaos_of(up, block), chaos_of(down, block)
    next_c = chaos_of(s, lax.rem(block + 1, GROUPS))
    prev_c = chaos_of(s, lax.rem(block + GROUPS - 1, GROUPS))

    barrier = pltpu.get_barrier_semaphore()
    peers = [(s, lax.rem(c + d, GROUPS)) for d in range(1, GROUPS)]
    peers += [(up, c), (down, c), (up, up_c), (down, down_c)]
    for peer in peers:
        pl.semaphore_signal(barrier, inc=1, device_id=peer, device_id_type=MESH)

    loads = [
        pltpu.make_async_copy(src, dst, load_sem.at[i])
        for i, (src, dst) in enumerate(((sol_ref, vsol), (kl_ref, vkl), (mean_ref, vmean), (mi_ref, vmi)))
    ]
    for load in loads:
        load.start()

    loads[0].wait()

    @pl.loop(0, MODES, unroll=4)
    def _(i):
        for t in range(4):
            rows = pl.ds(8 * t, 8)
            low, high = halves(vsol[i, 0, rows, :], vsol[i, 1, rows, :])
            send_v[2 * t, i] = low
            send_v[2 * t + 1, i] = high

    low4 = sublane() < 4
    sub4 = lax.rem(sublane(), 4)
    below_ok = s > 0
    above_ok = s < SLABS - 1
    has_next = block < GROUPS - 1
    has_prev = block > 0
    last_lane = lane() == 127

    first_lane = lane() == 0

    def planes(ref, at):
        return [ref[at, q] for q in range(5)]

    def term(f, g):
        return (f[0] * g[0] + f[1] * g[1]) + (f[3] * g[3] + f[4] * g[4]), f[2] * g[2]

    def gather(level, flux):
        return level + (flux - jnp.where(first_lane, 0.0, pltpu.roll(flux, 1, 1)))

    def mode_copy(d):
        target = lax.rem(c + d, GROUPS)
        return pltpu.make_async_remote_copy(
            send_v.at[block_of(s, target)],
            modes.at[pl.ds(c * MODES, MODES)],
            vs_sem.at[d],
            vr_sem.at[c],
            device_id=(s, target),
            device_id_type=MESH,
        )

    def field_copy(d):
        target = lax.rem(c + d, GROUPS)
        return pltpu.make_async_remote_copy(
            send_k.at[block_of(s, target)],
            fields.at[c],
            ks_sem.at[d],
            kr_sem.at[c],
            device_id=(s, target),
            device_id_type=MESH,
        )

    z_copies = [
        pltpu.make_async_remote_copy(
            src, dst, zs_sem.at[i], zr_sem.at[i], device_id=(up, c), device_id_type=MESH
        )
        for i, (src, dst) in enumerate(
            ((vkl.at[:, 2, 1], zface.at[pl.ds(0, FIELDS)]), (vmean.at[2, 1], zface.at[FIELDS]))
        )
    ]

    def send_faces_up():
        loads[2].wait()
        for copy in z_copies:
            copy.start()

    def send_modes():
        for d in range(1, GROUPS):
            mode_copy(d).start()

    def own_modes():
        @pl.loop(0, MODES, unroll=True)
        def _(i):
            modes[c * MODES + i] = send_v[block, i]

    def pack_fields():
        loads[1].wait()

        @pl.loop(0, FIELDS * 3, unroll=4)
        def _(q):
            k, dim = lax.div(q, 3), lax.rem(q, 3)
            for t in range(4):
                rows = pl.ds(8 * t, 8)
                low, high = halves(vkl[k, dim, 0, rows, :], vkl[k, dim, 1, rows, :])
                send_k[2 * t, q] = low
                send_k[2 * t + 1, q] = high

        for b in range(GROUPS):
            for k in range(FIELDS):
                for layer in range(2):
                    at = pl.ds(2 * k + layer, 1)
                    if b == 0:
                        send_k[b, FIELDS * 3, at, :] = jnp.zeros((1, 128), F32)
                    else:
                        send_k[b, FIELDS * 3, at, :] = vkl[k, 0, layer, pl.ds(4 * b - 1, 1), :]

    def pack_faces_below():
        for copy in z_copies:
            copy.wait()
        for pair in range(2):
            for t in range(4):
                rows = pl.ds(8 * t, 8)
                low, high = halves(zface[2 * pair, rows, :], zface[2 * pair + 1, rows, :])
                send_k[2 * t, FIELDS * 3 + 1 + pair] = low
                send_k[2 * t + 1, FIELDS * 3 + 1 + pair] = high

    def send_fields():
        for d in range(1, GROUPS):
            field_copy(d).start()

    def own_fields():
        @pl.loop(0, KL_TILES, unroll=True)
        def _(q):
            fields[c, q] = send_k[block, q]

    def halo_copies(group):
        cells = pl.ds(group * (MODES // 2), MODES // 2)
        targets = ((up, up_c), (down, down_c), (s, next_c), (s, prev_c))
        copies = []
        for i, target in enumerate(targets):
            source, buffer = (halo_src_z, halo_z) if i < 2 else (halo_src_x, halo_x)
            part = cells if i < 2 else group
            copies.append(
                pltpu.make_async_remote_copy(
                    source.at[i % 2, part],
                    buffer.at[i % 2, part],
                    hs_sem.at[i, group],
                    hr_sem.at[i, group],
                    device_id=target,
                    device_id_type=MESH,
                )
            )
        return copies

    def arrival(d):
        return lax.rem(c + GROUPS - d, GROUPS)

    def forward(group):
        @pl.loop(0, MODES // 2, unroll=True)
        def _(i):
            at = group * (MODES // 2) + i
            low, high = halves(modes[2 * at], modes[2 * at + 1])
            halo_src_z[0, at] = high
            halo_src_z[1, at] = low

        copies = halo_copies(group)
        copies[0].start()
        copies[1].start()
        for layer in range(2):
            for i in range(MODES):
                m = group * MODES + i
                at = pl.ds(i, 1)
                halo_src_x[0, group, layer, at, :] = modes[m, pl.ds(4 * layer + 3, 1), :]
                halo_src_x[1, group, layer, at, :] = modes[m, pl.ds(4 * layer, 1), :]
        pl.when(has_next)(copies[2].start)
        pl.when(has_prev)(copies[3].start)

    def forward_arrivals(first, last):
        @pl.loop(first, last)
        def _(d):
            group = arrival(d)
            pltpu.make_async_copy(send_v.at[0], modes.at[pl.ds(group * MODES, MODES)], vr_sem.at[group]).wait()
            forward(group)

    to_scalars = pltpu.make_async_copy(table, table_s, table_sem)

    def tables():
        loads[3].wait()
        make_tables(vmi, table)
        to_scalars.start()

    def mean_faces():
        for t in range(4):
            rows = pl.ds(8 * t, 8)
            parts = [halves(vmean[dim, 0, rows, :], vmean[dim, 1, rows, :]) for dim in range(3)]
            under = zface[FIELDS, rows, :]
            for h in range(2):
                b = 2 * t + h
                fx, fy, fz = (part[h] for part in parts)
                prior = pltpu.roll(fx, 1, 0)
                if b == 0:
                    prior = jnp.where(sub4 == 0, 0.0, prior)
                else:
                    edges = [row(vmean[0, layer, pl.ds(4 * b - 1, 1), :]) for layer in range(2)]
                    prior = jnp.where(sub4 == 0, jnp.where(low4, edges[0], edges[1]), prior)
                lower = under if h == 0 else pltpu.roll(under, 4, 0)
                lower = jnp.where(below_ok, lower, 0.0)
                for q, value in enumerate((fx, prior, fy, fz, jnp.where(low4, lower, pltpu.roll(fz, 4, 0)))):
                    mean_blocks[b, q] = value

    def differences(d):
        group = arrival(d)
        copies = halo_copies(group)
        copies[0].wait_recv()
        copies[1].wait_recv()
        pl.when(has_prev)(copies[2].wait_recv)
        pl.when(has_next)(copies[3].wait_recv)

        @pl.loop(0, MODES // 2, unroll=True)
        def _(i):
            cell = group * (MODES // 2) + i
            under = halo_z[0, cell]
            over = jnp.where(above_ok, halo_z[1, cell], 0.0)
            for odd in range(2):
                m = 2 * cell + odd
                at = pl.ds(2 * i + odd, 1)
                v = modes[m]
                before = jnp.where(low4, row(halo_x[0, group, 0, at, :]), row(halo_x[0, group, 1, at, :]))
                before = jnp.where(has_prev, before, 0.0)
                after = jnp.where(low4, row(halo_x[1, group, 0, at, :]), row(halo_x[1, group, 1, at, :]))
                after = jnp.where(has_next, after, 0.0)
                next_x = jnp.where(sub4 == 3, after, pltpu.roll(v, 7, 0))
                prev_x = jnp.where(sub4 == 0, before, pltpu.roll(v, 1, 0))
                next_y = jnp.where(last_lane, 0.0, pltpu.roll(v, 127, 1))
                swapped = pltpu.roll(v, 4, 0)
                next_z = jnp.where(low4, swapped, over if odd else pltpu.roll(over, 4, 0))
                prev_z = jnp.where(low4, pltpu.roll(under, 4, 0) if odd else under, swapped)
                steps = [v - other for other in (next_x, prev_x, next_y, next_z, prev_z)]
                for q, value in enumerate(steps):
                    diff[m, q] = value
                result[m] = gather(*term(planes(mean_blocks, block), steps))

    def faces(group):
        for k in range(FIELDS):
            fx, fy, fz = (fields[group, 3 * k + dim] for dim in range(3))
            edges = [row(fields[group, FIELDS * 3, pl.ds(2 * k + layer, 1), :]) for layer in range(2)]
            prior = jnp.where(sub4 == 0, jnp.where(low4, edges[0], edges[1]), pltpu.roll(fx, 1, 0))
            under = fields[group, FIELDS * 3 + 1 + k // 2]
            under = under if k % 2 == 0 else pltpu.roll(under, 4, 0)
            lower = jnp.where(low4, jnp.where(below_ok, under, 0.0), pltpu.roll(fz, 4, 0))
            for q, value in enumerate((fx, prior, fy, fz, lower)):
                face[group * FIELDS + k, q] = value

    def arrived_faces(first, last):
        @pl.loop(first, last)
        def _(d):
            group = arrival(d)
            pltpu.make_async_copy(send_k.at[0], fields.at[group], kr_sem.at[group]).wait()
            faces(group)

    def all_differences(first, last):
        pl.loop(first, last)(differences)

    pack_fields()
    own_modes()
    tables()
    pl.semaphore_wait(barrier, len(peers))
    send_faces_up()
    send_modes()
    forward(c)
    pack_faces_below()
    own_fields()
    mean_faces()
    forward_arrivals(1, GROUPS)
    send_fields()
    faces(c)
    all_differences(0, GROUPS)
    arrived_faces(1, GROUPS)
    to_scalars.wait()

    def result_copy(target):
        return pltpu.make_async_remote_copy(
            result.at[pl.ds(target * MODES, MODES)],
            out_ref.at[block],
            os_sem.at[target],
            or_sem.at[block],
            device_id=(s, target),
            device_id_type=MESH,
        )

    def send_result(target):
        pl.when(target != c)(lambda: result_copy(target).start())
        own = pltpu.make_async_copy(result.at[pl.ds(target * MODES, MODES)], out_ref.at[block], or_sem.at[block])
        pl.when(target == c)(own.start)

    def variables(p):
        code = table_s[2, 0, p]
        return code >> 7, (code >> 2) & (UNITS - 1), (code & 3) == 2

    def image(p):
        a, b, double = variables(p)
        raised = jnp.where(double, F32(ROOT2), F32(1.0))
        own = planes(diff, p)
        at = 2 * (p - FIRST_PAIR)
        images[at] = raised * gather(*term(planes(face, b), own))
        images[at + 1] = raised * gather(*term(planes(face, a), own))

    def pair(p):
        a, b, double = variables(p)
        weight = jnp.where(double, F32(0.5 * ROOT2), F32(1.0))
        level_a, flux_a = term(planes(face, a), planes(diff, 1 + b))
        level_b, flux_b = term(planes(face, b), planes(diff, 1 + a))
        result[p] = result[p] + weight * gather(level_a + level_b, flux_a + flux_b)

    pl.loop(FIRST_PAIR, TOTAL, unroll=IMAGE_UNROLL)(image)

    zero = jnp.zeros((8, 128), F32)
    sums[SLOTS] = zero
    run = SLOTS // RUNS

    @pl.loop(0, run, init_carry=((I32(-1), zero),) * RUNS, unroll=SLOT_UNROLL)
    def _(t, carry):
        now = []
        for r, (before, held) in enumerate(carry):
            at = t + r * run
            code = table_s[at >> 7, 0, at & (TOTAL - 1)]
            unit = code & (UNITS - 1)
            held = jnp.where(unit == before, held, 0.0) + images[code >> 5]
            sums[at] = held
            now.append((unit, held))
        return tuple(now)

    zeroth = planes(diff, 0)

    @pl.loop(0, UNITS, init_carry=(zero, zero), unroll=UNIT_UNROLL)
    def total(i, carry):
        field = planes(face, i)
        partial = sums[table_s[3, 0, i]] + sums[table_s[4, 0, i]]
        result[1 + i] = result[1 + i] + gather(*term(field, zeroth)) + partial
        level, flux = term(field, planes(diff, 1 + i))
        return carry[0] + level, carry[1] + flux

    result[0] = result[0] + gather(*total)

    pl.loop(FIRST_PAIR, FULL_GROUP * MODES, unroll=True)(pair)

    @pl.loop(1, GROUPS + 1)
    def _(d):
        target = out_peer(c, d)

        @pl.when(target >= FULL_GROUP)
        def _():
            @pl.loop(0, MODES, unroll=True)
            def _(i):
                pair(target * MODES + i)

        send_result(target)

    for b in range(GROUPS):
        pltpu.make_async_copy(result.at[pl.ds(0, MODES)], out_ref.at[b], or_sem.at[b]).wait()
    for d in range(1, GROUPS):
        mode_copy(d).wait_send()
        field_copy(d).wait_send()
        result_copy(peer_of(c, d)).wait_send()

    @pl.loop(0, GROUPS)
    def _(d):
        copies = halo_copies(arrival(d))
        copies[0].wait_send()
        copies[1].wait_send()
        pl.when(has_next)(copies[2].wait_send)
        pl.when(has_prev)(copies[3].wait_send)


def unpack(blocks_ref, out_ref):
    @pl.loop(0, MODES)
    def _(i):
        for t in range(4):
            rows = pl.ds(8 * t, 8)
            low, high = halves(blocks_ref[2 * t, i], blocks_ref[2 * t + 1, i])
            out_ref[i, 0, rows, :] = low
            out_ref[i, 1, rows, :] = high


def shards(sol, mean, kl, multi_index, couplings):
    tile = (8, 128)
    sem = pltpu.SemaphoreType.DMA
    blocks = pl.pallas_call(
        kernel,
        out_shape=jax.ShapeDtypeStruct((GROUPS, MODES) + tile, F32),
        in_specs=[pl.BlockSpec(memory_space=pltpu.HBM)] * 4,
        out_specs=pl.BlockSpec(memory_space=pl.ANY),
        scratch_shapes=[
            pltpu.VMEM((MODES, 2, 32, 128), F32),
            pltpu.VMEM((3, 2, 32, 128), F32),
            pltpu.VMEM((FIELDS, 3, 2, 32, 128), F32),
            pltpu.VMEM((UNITS, TOTAL), I32),
            pltpu.VMEM((GROUPS, MODES) + tile, F32),
            pltpu.VMEM((GROUPS, KL_TILES) + tile, F32),
            pltpu.VMEM((TOTAL,) + tile, F32),
            pltpu.VMEM((GROUPS, KL_TILES) + tile, F32),
            pltpu.VMEM((FIELDS + 1, 32, 128), F32),
            pltpu.VMEM((GROUPS, 5) + tile, F32),
            pltpu.VMEM((2, TOTAL // 2) + tile, F32),
            pltpu.VMEM((2, GROUPS, 2, MODES, 128), F32),
            pltpu.VMEM((2, TOTAL // 2) + tile, F32),
            pltpu.VMEM((2, GROUPS, 2, MODES, 128), F32),
            pltpu.VMEM((TOTAL, 5) + tile, F32),
            pltpu.VMEM((UNITS, 5) + tile, F32),
            pltpu.VMEM((SLOTS,) + tile, F32),
            pltpu.VMEM((SLOTS + 1,) + tile, F32),
            pltpu.VMEM((TOTAL,) + tile, F32),
            pltpu.VMEM((5,) + tile, I32),
            pltpu.SMEM((5,) + tile, I32),
            sem((4,)),
            sem((GROUPS,)),
            sem((GROUPS,)),
            sem((GROUPS,)),
            sem((GROUPS,)),
            sem((2,)),
            sem((2,)),
            sem((4, GROUPS)),
            sem((4, GROUPS)),
            sem((GROUPS,)),
            sem((GROUPS,)),
            sem,
        ],
        compiler_params=pltpu.CompilerParams(
            collective_id=0, has_side_effects=True, vmem_limit_bytes=60 * 2**20
        ),
        name="apply",
    )(sol, mean, kl, multi_index.T)
    return pl.pallas_call(
        unpack,
        out_shape=jax.ShapeDtypeStruct((MODES, 2, 32, 128), F32),
        in_specs=[pl.BlockSpec(memory_space=pltpu.VMEM)],
        out_specs=pl.BlockSpec(memory_space=pltpu.VMEM),
        name="unpack",
    )(blocks)


def solution(mesh):
    return jax.shard_map(
        shards,
        mesh=mesh,
        in_specs=(
            P("chaos", "space", None, None),
            P(None, "space", None, None),
            P("chaos", None, "space", None, None),
            P(),
            P(),
        ),
        out_specs=P("chaos", "space", None, None),
        check_vma=False,
    )
```

```python
import math

import jax
import jax.numpy as jnp
from jax import lax
from jax.experimental import pallas as pl
from jax.experimental.pallas import tpu as pltpu
from jax.sharding import PartitionSpec as P

MESH = pl.DeviceIdType.MESH
F32 = jnp.float32
I32 = jnp.int32
SLABS = 16
GROUPS = 8
MODES = 16
FIELDS = 4
KL_TILES = FIELDS * 3 + 3
UNITS = 32
FIRST_PAIR = 33
TOTAL = 128
SLOTS = 192
FULL_GROUP = 3
IMAGE_UNROLL = 95
SLOT_UNROLL = 48
RUNS = 4
UNIT_UNROLL = 32
ROOT2 = math.sqrt(2.0)


def flip_of(slab):
    return lax.rem(lax.div(slab, 4), 2)


def block_of(slab, chaos):
    high = lax.rem(lax.div(chaos, 4) + flip_of(slab), 2)
    y = lax.rem(lax.rem(chaos, 4) + 1, 4)
    return high * 4 + high * (3 - y) + (1 - high) * y


def chaos_of(slab, block):
    high = lax.div(block, 4)
    low = lax.rem(block, 4)
    y = lax.rem(high * (3 - low) + (1 - high) * low + 3, 4)
    return lax.rem(high + flip_of(slab), 2) * 4 + y


def peer_of(chaos, d):
    high = lax.rem(lax.div(chaos, 4) + lax.div(d, 4), 2)
    return high * 4 + lax.rem(lax.rem(chaos, 4) + lax.rem(d, 4), 4)


def source_of(chaos, d):
    high = lax.rem(lax.div(chaos, 4) + lax.div(d, 4), 2)
    return high * 4 + lax.rem(lax.rem(chaos, 4) + 4 - lax.rem(d, 4), 4)


def out_peer(chaos, d):
    d = lax.rem(d, 8)
    move = d * 0
    move = move + jnp.where(d == 1, 6, 0)
    move = move + jnp.where(d == 2, 2, 0)
    move = move + jnp.where(d == 3, 5, 0)
    move = move + jnp.where(d == 4, 7, 0)
    move = move + jnp.where(d == 5, 4, 0)
    move = move + jnp.where(d == 6, 1, 0)
    move = move + jnp.where(d == 7, 3, 0)
    high = lax.rem(lax.div(chaos, 4) + lax.div(move, 4), 2)
    return high * 4 + lax.rem(lax.rem(chaos, 4) + lax.rem(move, 4), 4)


def in_peer(chaos, d):
    d = lax.rem(d, 8)
    move = d * 0
    move = move + jnp.where(d == 1, 6, 0)
    move = move + jnp.where(d == 2, 2, 0)
    move = move + jnp.where(d == 3, 5, 0)
    move = move + jnp.where(d == 4, 7, 0)
    move = move + jnp.where(d == 5, 4, 0)
    move = move + jnp.where(d == 6, 1, 0)
    move = move + jnp.where(d == 7, 3, 0)
    high = lax.rem(lax.div(chaos, 4) + lax.div(move, 4), 2)
    return high * 4 + lax.rem(lax.rem(chaos, 4) + lax.rem(move, 4), 4)


def in_source(chaos, d):
    d = lax.rem(d, 8)
    move = d * 0
    move = move + jnp.where(d == 1, 6, 0)
    move = move + jnp.where(d == 2, 2, 0)
    move = move + jnp.where(d == 3, 5, 0)
    move = move + jnp.where(d == 4, 7, 0)
    move = move + jnp.where(d == 5, 4, 0)
    move = move + jnp.where(d == 6, 1, 0)
    move = move + jnp.where(d == 7, 3, 0)
    high = lax.rem(lax.div(chaos, 4) + lax.div(move, 4), 2)
    return high * 4 + lax.rem(lax.rem(chaos, 4) + 4 - lax.rem(move, 4), 4)


def sublane():
    return lax.broadcasted_iota(I32, (8, 128), 0)


def lane():
    return lax.broadcasted_iota(I32, (8, 128), 1)


def halves(a, b):
    low = sublane() < 4
    return jnp.where(low, a, pltpu.roll(b, 4, 0)), jnp.where(low, pltpu.roll(a, 4, 0), b)


def row(ref_row):
    return jnp.broadcast_to(ref_row, (8, 128))


def make_tables(mi_ref, table_ref):
    shape = (TOTAL, TOTAL)
    mode = lax.broadcasted_iota(I32, shape, 0)
    var = lax.broadcasted_iota(I32, shape, 1)
    degree = jnp.concatenate([mi_ref[...], jnp.zeros((TOTAL - UNITS, TOTAL), I32)], axis=0).T
    is_pair = mode >= FIRST_PAIR
    held = (degree > 0) & is_pair
    count = held.astype(I32)
    running = count
    step = 1
    while step < TOTAL:
        running = running + jnp.where(mode >= step, pltpu.roll(running, step, 0), 0)
        step *= 2
    total = jnp.broadcast_to(running[TOTAL - 1 :, :], (8, TOTAL))
    var8 = lax.broadcasted_iota(I32, (8, TOTAL), 1)
    prefix = total
    step = 1
    while step < UNITS:
        prefix = prefix + jnp.where(var8 >= step, pltpu.roll(prefix, step, 1), 0)
        step *= 2
    start = prefix - total
    place = running - count + jnp.broadcast_to(start[:1, :], shape)
    first = jnp.min(jnp.where(held, var, TOTAL), axis=1, keepdims=True)
    last = jnp.max(jnp.where(held, var, -1), axis=1, keepdims=True)
    place_a = jnp.max(jnp.where(held & (var == first), place, -1), axis=1, keepdims=True)
    place_b = jnp.max(jnp.where(held & (var == last), place, -1), axis=1, keepdims=True)
    column = lax.broadcasted_iota(I32, (TOTAL, 1), 0)
    pair = column >= FIRST_PAIR
    double = first == last
    kind = jnp.where(double, 2, 1)
    first = jnp.where(pair, jnp.minimum(first, UNITS - 1), 0)
    last = jnp.where(pair, jnp.maximum(last, 0), 0)
    code_a = jnp.where(pair, (column - FIRST_PAIR) * 2 * UNITS + first, 0)
    code_b = jnp.where(pair & jnp.logical_not(double), ((column - FIRST_PAIR) * 2 + 1) * UNITS + last, 0)
    code_p = (first * UNITS + last) * 4 + kind
    for half in range(2):
        slot = var + half * TOTAL
        code = jnp.where(place_a == slot, code_a, 0) + jnp.where(place_b == slot, code_b, 0)
        table_ref[half] = jnp.broadcast_to(jnp.sum(code, axis=0, keepdims=True), (8, TOTAL))
    table_ref[2] = jnp.broadcast_to(
        jnp.sum(jnp.where(mode == var, code_p, 0), axis=0, keepdims=True), (8, TOTAL)
    )
    end = prefix - 1
    run = SLOTS // RUNS
    first_run = sum((start >= r * run).astype(I32) for r in range(1, RUNS))
    last_run = sum((end >= r * run).astype(I32) for r in range(1, RUNS))
    table_ref[3] = jnp.where(total > 0, end, SLOTS)
    table_ref[4] = jnp.where((total > 0) & (last_run > first_run), last_run * run - 1, SLOTS)


def kernel(
    sol_ref, mean_ref, kl_ref, mi_ref, out_ref,
    vsol, vmean, vkl, vmi, send_v, send_k, modes, fields, zface, mean_blocks,
    halo_src_z, halo_src_x, halo_z, halo_x, diff, face, images, sums, result, table, table_s,
    load_sem, vs_sem, vr_sem, ks_sem, kr_sem, zs_sem, zr_sem, hs_sem, hr_sem, os_sem, or_sem, table_sem,
):
    s, c = lax.axis_index("space"), lax.axis_index("chaos")
    up, down = lax.rem(s + 1, SLABS), lax.rem(s + SLABS - 1, SLABS)
    block = block_of(s, c)
    up_c, down_c = chaos_of(up, block), chaos_of(down, block)
    next_c = chaos_of(s, lax.rem(block + 1, GROUPS))
    prev_c = chaos_of(s, lax.rem(block + GROUPS - 1, GROUPS))

    barrier = pltpu.get_barrier_semaphore()
    peers = [(s, lax.rem(c + d, GROUPS)) for d in range(1, GROUPS)]
    peers += [(up, c), (down, c), (up, up_c), (down, down_c)]
    for peer in peers:
        pl.semaphore_signal(barrier, inc=1, device_id=peer, device_id_type=MESH)

    loads = [
        pltpu.make_async_copy(src, dst, load_sem.at[i])
        for i, (src, dst) in enumerate(((sol_ref, vsol), (kl_ref, vkl), (mean_ref, vmean), (mi_ref, vmi)))
    ]
    for load in loads:
        load.start()

    loads[0].wait()

    @pl.loop(0, MODES, unroll=4)
    def _(i):
        for t in range(4):
            rows = pl.ds(8 * t, 8)
            low, high = halves(vsol[i, 0, rows, :], vsol[i, 1, rows, :])
            send_v[2 * t, i] = low
            send_v[2 * t + 1, i] = high

    low4 = sublane() < 4
    sub4 = lax.rem(sublane(), 4)
    below_ok = s > 0
    above_ok = s < SLABS - 1
    has_next = block < GROUPS - 1
    has_prev = block > 0
    last_lane = lane() == 127

    first_lane = lane() == 0

    def planes(ref, at):
        return [ref[at, q] for q in range(5)]

    def term(f, g):
        return (f[0] * g[0] + f[1] * g[1]) + (f[3] * g[3] + f[4] * g[4]), f[2] * g[2]

    def gather(level, flux):
        return level + (flux - jnp.where(first_lane, 0.0, pltpu.roll(flux, 1, 1)))

    def mode_copy(d):
        target = in_peer(c, d)
        return pltpu.make_async_remote_copy(
            send_v.at[block_of(s, target)],
            modes.at[pl.ds(c * MODES, MODES)],
            vs_sem.at[d],
            vr_sem.at[c],
            device_id=(s, target),
            device_id_type=MESH,
        )

    def field_copy(d):
        target = in_peer(c, d)
        return pltpu.make_async_remote_copy(
            send_k.at[block_of(s, target)],
            fields.at[c],
            ks_sem.at[d],
            kr_sem.at[c],
            device_id=(s, target),
            device_id_type=MESH,
        )

    z_copies = [
        pltpu.make_async_remote_copy(
            src, dst, zs_sem.at[i], zr_sem.at[i], device_id=(up, c), device_id_type=MESH
        )
        for i, (src, dst) in enumerate(
            ((vkl.at[:, 2, 1], zface.at[pl.ds(0, FIELDS)]), (vmean.at[2, 1], zface.at[FIELDS]))
        )
    ]

    def send_faces_up():
        loads[1].wait()
        loads[2].wait()
        for copy in z_copies:
            copy.start()

    def send_modes():
        for d in range(1, GROUPS):
            mode_copy(d).start()

    def own_modes():
        @pl.loop(0, MODES, unroll=True)
        def _(i):
            modes[c * MODES + i] = send_v[block, i]

    def pack_fields():
        @pl.loop(0, FIELDS * 3, unroll=4)
        def _(q):
            k, dim = lax.div(q, 3), lax.rem(q, 3)
            for t in range(4):
                rows = pl.ds(8 * t, 8)
                low, high = halves(vkl[k, dim, 0, rows, :], vkl[k, dim, 1, rows, :])
                send_k[2 * t, q] = low
                send_k[2 * t + 1, q] = high

        for b in range(GROUPS):
            for k in range(FIELDS):
                for layer in range(2):
                    at = pl.ds(2 * k + layer, 1)
                    if b == 0:
                        send_k[b, FIELDS * 3, at, :] = jnp.zeros((1, 128), F32)
                    else:
                        send_k[b, FIELDS * 3, at, :] = vkl[k, 0, layer, pl.ds(4 * b - 1, 1), :]

    def pack_faces_below():
        for copy in z_copies:
            copy.wait()
        for pair in range(2):
            for t in range(4):
                rows = pl.ds(8 * t, 8)
                low, high = halves(zface[2 * pair, rows, :], zface[2 * pair + 1, rows, :])
                send_k[2 * t, FIELDS * 3 + 1 + pair] = low
                send_k[2 * t + 1, FIELDS * 3 + 1 + pair] = high

    def send_fields():
        for d in range(1, GROUPS):
            field_copy(d).start()

    def own_fields():
        @pl.loop(0, KL_TILES, unroll=True)
        def _(q):
            fields[c, q] = send_k[block, q]

    def halo_copies(group):
        cells = pl.ds(group * (MODES // 2), MODES // 2)
        targets = ((up, up_c), (down, down_c), (s, next_c), (s, prev_c))
        copies = []
        for i, target in enumerate(targets):
            source, buffer = (halo_src_z, halo_z) if i < 2 else (halo_src_x, halo_x)
            part = cells if i < 2 else group
            copies.append(
                pltpu.make_async_remote_copy(
                    source.at[i % 2, part],
                    buffer.at[i % 2, part],
                    hs_sem.at[i, group],
                    hr_sem.at[i, group],
                    device_id=target,
                    device_id_type=MESH,
                )
            )
        return copies

    def arrival(d):
        return in_source(c, d)

    def forward(group):
        @pl.loop(0, MODES // 2, unroll=True)
        def _(i):
            at = group * (MODES // 2) + i
            low, high = halves(modes[2 * at], modes[2 * at + 1])
            halo_src_z[0, at] = high
            halo_src_z[1, at] = low

        copies = halo_copies(group)
        copies[0].start()
        copies[1].start()
        for layer in range(2):
            for i in range(MODES):
                m = group * MODES + i
                at = pl.ds(i, 1)
                halo_src_x[0, group, layer, at, :] = modes[m, pl.ds(4 * layer + 3, 1), :]
                halo_src_x[1, group, layer, at, :] = modes[m, pl.ds(4 * layer, 1), :]
        pl.when(has_next)(copies[2].start)
        pl.when(has_prev)(copies[3].start)

    def forward_arrivals(first, last):
        @pl.loop(first, last)
        def _(d):
            group = arrival(d)
            pltpu.make_async_copy(send_v.at[0], modes.at[pl.ds(group * MODES, MODES)], vr_sem.at[group]).wait()
            forward(group)

    to_scalars = pltpu.make_async_copy(table, table_s, table_sem)

    def tables():
        loads[3].wait()
        make_tables(vmi, table)
        to_scalars.start()

    def mean_faces():
        for t in range(4):
            rows = pl.ds(8 * t, 8)
            parts = [halves(vmean[dim, 0, rows, :], vmean[dim, 1, rows, :]) for dim in range(3)]
            under = zface[FIELDS, rows, :]
            for h in range(2):
                b = 2 * t + h
                fx, fy, fz = (part[h] for part in parts)
                prior = pltpu.roll(fx, 1, 0)
                if b == 0:
                    prior = jnp.where(sub4 == 0, 0.0, prior)
                else:
                    edges = [row(vmean[0, layer, pl.ds(4 * b - 1, 1), :]) for layer in range(2)]
                    prior = jnp.where(sub4 == 0, jnp.where(low4, edges[0], edges[1]), prior)
                lower = under if h == 0 else pltpu.roll(under, 4, 0)
                lower = jnp.where(below_ok, lower, 0.0)
                for q, value in enumerate((fx, prior, fy, fz, jnp.where(low4, lower, pltpu.roll(fz, 4, 0)))):
                    mean_blocks[b, q] = value

    def differences(d):
        group = arrival(d)
        copies = halo_copies(group)
        copies[0].wait_recv()
        copies[1].wait_recv()
        pl.when(has_prev)(copies[2].wait_recv)
        pl.when(has_next)(copies[3].wait_recv)

        @pl.loop(0, MODES // 2, unroll=True)
        def _(i):
            cell = group * (MODES // 2) + i
            under = halo_z[0, cell]
            over = jnp.where(above_ok, halo_z[1, cell], 0.0)
            for odd in range(2):
                m = 2 * cell + odd
                at = pl.ds(2 * i + odd, 1)
                v = modes[m]
                before = jnp.where(low4, row(halo_x[0, group, 0, at, :]), row(halo_x[0, group, 1, at, :]))
                before = jnp.where(has_prev, before, 0.0)
                after = jnp.where(low4, row(halo_x[1, group, 0, at, :]), row(halo_x[1, group, 1, at, :]))
                after = jnp.where(has_next, after, 0.0)
                next_x = jnp.where(sub4 == 3, after, pltpu.roll(v, 7, 0))
                prev_x = jnp.where(sub4 == 0, before, pltpu.roll(v, 1, 0))
                next_y = jnp.where(last_lane, 0.0, pltpu.roll(v, 127, 1))
                swapped = pltpu.roll(v, 4, 0)
                next_z = jnp.where(low4, swapped, over if odd else pltpu.roll(over, 4, 0))
                prev_z = jnp.where(low4, pltpu.roll(under, 4, 0) if odd else under, swapped)
                steps = [v - other for other in (next_x, prev_x, next_y, next_z, prev_z)]
                for q, value in enumerate(steps):
                    diff[m, q] = value
                result[m] = gather(*term(planes(mean_blocks, block), steps))

    def faces(group):
        for k in range(FIELDS):
            fx, fy, fz = (fields[group, 3 * k + dim] for dim in range(3))
            edges = [row(fields[group, FIELDS * 3, pl.ds(2 * k + layer, 1), :]) for layer in range(2)]
            prior = jnp.where(sub4 == 0, jnp.where(low4, edges[0], edges[1]), pltpu.roll(fx, 1, 0))
            under = fields[group, FIELDS * 3 + 1 + k // 2]
            under = under if k % 2 == 0 else pltpu.roll(under, 4, 0)
            lower = jnp.where(low4, jnp.where(below_ok, under, 0.0), pltpu.roll(fz, 4, 0))
            for q, value in enumerate((fx, prior, fy, fz, lower)):
                face[group * FIELDS + k, q] = value

    def arrived_faces(first, last):
        @pl.loop(first, last)
        def _(d):
            group = arrival(d)
            pltpu.make_async_copy(send_k.at[0], fields.at[group], kr_sem.at[group]).wait()
            faces(group)

    def all_differences(first, last):
        pl.loop(first, last)(differences)

    pl.semaphore_wait(barrier, len(peers))
    send_modes()
    own_modes()
    forward(c)
    send_faces_up()
    pack_fields()
    tables()
    forward_arrivals(1, GROUPS)
    pack_faces_below()
    send_fields()
    own_fields()
    mean_faces()
    faces(c)
    all_differences(0, GROUPS)
    arrived_faces(1, GROUPS)
    to_scalars.wait()

    def result_copy(target):
        return pltpu.make_async_remote_copy(
            result.at[pl.ds(target * MODES, MODES)],
            out_ref.at[block],
            os_sem.at[target],
            or_sem.at[block],
            device_id=(s, target),
            device_id_type=MESH,
        )

    def send_result(target):
        pl.when(target != c)(lambda: result_copy(target).start())
        own = pltpu.make_async_copy(result.at[pl.ds(target * MODES, MODES)], out_ref.at[block], or_sem.at[block])
        pl.when(target == c)(own.start)

    def variables(p):
        code = table_s[2, 0, p]
        return code >> 7, (code >> 2) & (UNITS - 1), (code & 3) == 2

    def image(p):
        a, b, double = variables(p)
        raised = jnp.where(double, F32(ROOT2), F32(1.0))
        own = planes(diff, p)
        at = 2 * (p - FIRST_PAIR)
        images[at] = raised * gather(*term(planes(face, b), own))
        images[at + 1] = raised * gather(*term(planes(face, a), own))

    def pair(p):
        a, b, double = variables(p)
        weight = jnp.where(double, F32(0.5 * ROOT2), F32(1.0))
        level_a, flux_a = term(planes(face, a), planes(diff, 1 + b))
        level_b, flux_b = term(planes(face, b), planes(diff, 1 + a))
        result[p] = result[p] + weight * gather(level_a + level_b, flux_a + flux_b)

    pl.loop(FIRST_PAIR, TOTAL, unroll=IMAGE_UNROLL)(image)

    zero = jnp.zeros((8, 128), F32)
    sums[SLOTS] = zero
    run = SLOTS // RUNS

    @pl.loop(0, run, init_carry=((I32(-1), zero),) * RUNS, unroll=SLOT_UNROLL)
    def _(t, carry):
        now = []
        for r, (before, held) in enumerate(carry):
            at = t + r * run
            code = table_s[at >> 7, 0, at & (TOTAL - 1)]
            unit = code & (UNITS - 1)
            held = jnp.where(unit == before, held, 0.0) + images[code >> 5]
            sums[at] = held
            now.append((unit, held))
        return tuple(now)

    zeroth = planes(diff, 0)

    @pl.loop(0, UNITS, init_carry=(zero, zero), unroll=UNIT_UNROLL)
    def total(i, carry):
        field = planes(face, i)
        partial = sums[table_s[3, 0, i]] + sums[table_s[4, 0, i]]
        result[1 + i] = result[1 + i] + gather(*term(field, zeroth)) + partial
        level, flux = term(field, planes(diff, 1 + i))
        return carry[0] + level, carry[1] + flux

    result[0] = result[0] + gather(*total)

    pl.loop(FIRST_PAIR, FULL_GROUP * MODES, unroll=True)(pair)

    @pl.loop(1, GROUPS + 1)
    def _(d):
        target = out_peer(c, d)

        @pl.when(target >= FULL_GROUP)
        def _():
            @pl.loop(0, MODES, unroll=True)
            def _(i):
                pair(target * MODES + i)

        send_result(target)

    for b in range(GROUPS):
        pltpu.make_async_copy(result.at[pl.ds(0, MODES)], out_ref.at[b], or_sem.at[b]).wait()
    for d in range(1, GROUPS):
        mode_copy(d).wait_send()
        field_copy(d).wait_send()
        result_copy(peer_of(c, d)).wait_send()

    @pl.loop(0, GROUPS)
    def _(d):
        copies = halo_copies(arrival(d))
        copies[0].wait_send()
        copies[1].wait_send()
        pl.when(has_next)(copies[2].wait_send)
        pl.when(has_prev)(copies[3].wait_send)


def unpack(blocks_ref, out_ref):
    @pl.loop(0, MODES)
    def _(i):
        for t in range(4):
            rows = pl.ds(8 * t, 8)
            low, high = halves(blocks_ref[2 * t, i], blocks_ref[2 * t + 1, i])
            out_ref[i, 0, rows, :] = low
            out_ref[i, 1, rows, :] = high


def shards(sol, mean, kl, multi_index, couplings):
    tile = (8, 128)
    sem = pltpu.SemaphoreType.DMA
    blocks = pl.pallas_call(
        kernel,
        out_shape=jax.ShapeDtypeStruct((GROUPS, MODES) + tile, F32),
        in_specs=[pl.BlockSpec(memory_space=pltpu.HBM)] * 4,
        out_specs=pl.BlockSpec(memory_space=pl.ANY),
        scratch_shapes=[
            pltpu.VMEM((MODES, 2, 32, 128), F32),
            pltpu.VMEM((3, 2, 32, 128), F32),
            pltpu.VMEM((FIELDS, 3, 2, 32, 128), F32),
            pltpu.VMEM((UNITS, TOTAL), I32),
            pltpu.VMEM((GROUPS, MODES) + tile, F32),
            pltpu.VMEM((GROUPS, KL_TILES) + tile, F32),
            pltpu.VMEM((TOTAL,) + tile, F32),
            pltpu.VMEM((GROUPS, KL_TILES) + tile, F32),
            pltpu.VMEM((FIELDS + 1, 32, 128), F32),
            pltpu.VMEM((GROUPS, 5) + tile, F32),
            pltpu.VMEM((2, TOTAL // 2) + tile, F32),
            pltpu.VMEM((2, GROUPS, 2, MODES, 128), F32),
            pltpu.VMEM((2, TOTAL // 2) + tile, F32),
            pltpu.VMEM((2, GROUPS, 2, MODES, 128), F32),
            pltpu.VMEM((TOTAL, 5) + tile, F32),
            pltpu.VMEM((UNITS, 5) + tile, F32),
            pltpu.VMEM((SLOTS,) + tile, F32),
            pltpu.VMEM((SLOTS + 1,) + tile, F32),
            pltpu.VMEM((TOTAL,) + tile, F32),
            pltpu.VMEM((5,) + tile, I32),
            pltpu.SMEM((5,) + tile, I32),
            sem((4,)),
            sem((GROUPS,)),
            sem((GROUPS,)),
            sem((GROUPS,)),
            sem((GROUPS,)),
            sem((2,)),
            sem((2,)),
            sem((4, GROUPS)),
            sem((4, GROUPS)),
            sem((GROUPS,)),
            sem((GROUPS,)),
            sem,
        ],
        compiler_params=pltpu.CompilerParams(
            collective_id=0, has_side_effects=True, vmem_limit_bytes=60 * 2**20
        ),
        name="apply",
    )(sol, mean, kl, multi_index.T)
    return pl.pallas_call(
        unpack,
        out_shape=jax.ShapeDtypeStruct((MODES, 2, 32, 128), F32),
        in_specs=[pl.BlockSpec(memory_space=pltpu.VMEM)],
        out_specs=pl.BlockSpec(memory_space=pltpu.VMEM),
        name="unpack",
    )(blocks)


def solution(mesh):
    return jax.shard_map(
        shards,
        mesh=mesh,
        in_specs=(
            P("chaos", "space", None, None),
            P(None, "space", None, None),
            P("chaos", None, "space", None, None),
            P(),
            P(),
        ),
        out_specs=P("chaos", "space", None, None),
        check_vma=False,
    )
```

```python
import math

import jax
import jax.numpy as jnp
from jax import lax
from jax.experimental import pallas as pl
from jax.experimental.pallas import tpu as pltpu
from jax.sharding import PartitionSpec as P

MESH = pl.DeviceIdType.MESH
F32 = jnp.float32
I32 = jnp.int32
SLABS = 16
GROUPS = 8
MODES = 16
FIELDS = 4
KL_TILES = FIELDS * 3 + 3
UNITS = 32
FIRST_PAIR = 33
TOTAL = 128
SLOTS = 192
FULL_GROUP = 3
IMAGE_UNROLL = 95
SLOT_UNROLL = 48
RUNS = 4
UNIT_UNROLL = 32
ROOT2 = math.sqrt(2.0)


def flip_of(slab):
    return lax.rem(lax.div(slab, 4), 2)


def block_of(slab, chaos):
    high = lax.rem(lax.div(chaos, 4) + flip_of(slab), 2)
    y = lax.rem(lax.rem(chaos, 4) + 1, 4)
    return high * 4 + high * (3 - y) + (1 - high) * y


def chaos_of(slab, block):
    high = lax.div(block, 4)
    low = lax.rem(block, 4)
    y = lax.rem(high * (3 - low) + (1 - high) * low + 3, 4)
    return lax.rem(high + flip_of(slab), 2) * 4 + y


def peer_of(chaos, d):
    high = lax.rem(lax.div(chaos, 4) + lax.div(d, 4), 2)
    return high * 4 + lax.rem(lax.rem(chaos, 4) + lax.rem(d, 4), 4)


def source_of(chaos, d):
    high = lax.rem(lax.div(chaos, 4) + lax.div(d, 4), 2)
    return high * 4 + lax.rem(lax.rem(chaos, 4) + 4 - lax.rem(d, 4), 4)


def out_peer(chaos, d):
    d = lax.rem(d, 8)
    move = d * 0
    move = move + jnp.where(d == 1, 6, 0)
    move = move + jnp.where(d == 2, 2, 0)
    move = move + jnp.where(d == 3, 5, 0)
    move = move + jnp.where(d == 4, 7, 0)
    move = move + jnp.where(d == 5, 4, 0)
    move = move + jnp.where(d == 6, 1, 0)
    move = move + jnp.where(d == 7, 3, 0)
    high = lax.rem(lax.div(chaos, 4) + lax.div(move, 4), 2)
    return high * 4 + lax.rem(lax.rem(chaos, 4) + lax.rem(move, 4), 4)


def in_peer(chaos, d):
    d = lax.rem(d, 8)
    move = d * 0
    move = move + jnp.where(d == 1, 6, 0)
    move = move + jnp.where(d == 2, 2, 0)
    move = move + jnp.where(d == 3, 5, 0)
    move = move + jnp.where(d == 4, 7, 0)
    move = move + jnp.where(d == 5, 4, 0)
    move = move + jnp.where(d == 6, 1, 0)
    move = move + jnp.where(d == 7, 3, 0)
    high = lax.rem(lax.div(chaos, 4) + lax.div(move, 4), 2)
    return high * 4 + lax.rem(lax.rem(chaos, 4) + lax.rem(move, 4), 4)


def in_source(chaos, d):
    d = lax.rem(d, 8)
    move = d * 0
    move = move + jnp.where(d == 1, 6, 0)
    move = move + jnp.where(d == 2, 2, 0)
    move = move + jnp.where(d == 3, 5, 0)
    move = move + jnp.where(d == 4, 7, 0)
    move = move + jnp.where(d == 5, 4, 0)
    move = move + jnp.where(d == 6, 1, 0)
    move = move + jnp.where(d == 7, 3, 0)
    high = lax.rem(lax.div(chaos, 4) + lax.div(move, 4), 2)
    return high * 4 + lax.rem(lax.rem(chaos, 4) + 4 - lax.rem(move, 4), 4)


def sublane():
    return lax.broadcasted_iota(I32, (8, 128), 0)


def lane():
    return lax.broadcasted_iota(I32, (8, 128), 1)


def halves(a, b):
    low = sublane() < 4
    return jnp.where(low, a, pltpu.roll(b, 4, 0)), jnp.where(low, pltpu.roll(a, 4, 0), b)


def row(ref_row):
    return jnp.broadcast_to(ref_row, (8, 128))


def make_tables(mi_ref, table_ref):
    shape = (TOTAL, TOTAL)
    mode = lax.broadcasted_iota(I32, shape, 0)
    var = lax.broadcasted_iota(I32, shape, 1)
    degree = jnp.concatenate([mi_ref[...], jnp.zeros((TOTAL - UNITS, TOTAL), I32)], axis=0).T
    is_pair = mode >= FIRST_PAIR
    held = (degree > 0) & is_pair
    count = held.astype(I32)
    running = count
    step = 1
    while step < TOTAL:
        running = running + jnp.where(mode >= step, pltpu.roll(running, step, 0), 0)
        step *= 2
    total = jnp.broadcast_to(running[TOTAL - 1 :, :], (8, TOTAL))
    var8 = lax.broadcasted_iota(I32, (8, TOTAL), 1)
    prefix = total
    step = 1
    while step < UNITS:
        prefix = prefix + jnp.where(var8 >= step, pltpu.roll(prefix, step, 1), 0)
        step *= 2
    start = prefix - total
    place = running - count + jnp.broadcast_to(start[:1, :], shape)
    first = jnp.min(jnp.where(held, var, TOTAL), axis=1, keepdims=True)
    last = jnp.max(jnp.where(held, var, -1), axis=1, keepdims=True)
    place_a = jnp.max(jnp.where(held & (var == first), place, -1), axis=1, keepdims=True)
    place_b = jnp.max(jnp.where(held & (var == last), place, -1), axis=1, keepdims=True)
    column = lax.broadcasted_iota(I32, (TOTAL, 1), 0)
    pair = column >= FIRST_PAIR
    double = first == last
    kind = jnp.where(double, 2, 1)
    first = jnp.where(pair, jnp.minimum(first, UNITS - 1), 0)
    last = jnp.where(pair, jnp.maximum(last, 0), 0)
    code_a = jnp.where(pair, (column - FIRST_PAIR) * 2 * UNITS + first, 0)
    code_b = jnp.where(pair & jnp.logical_not(double), ((column - FIRST_PAIR) * 2 + 1) * UNITS + last, 0)
    code_p = (first * UNITS + last) * 4 + kind
    for half in range(2):
        slot = var + half * TOTAL
        code = jnp.where(place_a == slot, code_a, 0) + jnp.where(place_b == slot, code_b, 0)
        table_ref[half] = jnp.broadcast_to(jnp.sum(code, axis=0, keepdims=True), (8, TOTAL))
    table_ref[2] = jnp.broadcast_to(
        jnp.sum(jnp.where(mode == var, code_p, 0), axis=0, keepdims=True), (8, TOTAL)
    )
    end = prefix - 1
    run = SLOTS // RUNS
    first_run = sum((start >= r * run).astype(I32) for r in range(1, RUNS))
    last_run = sum((end >= r * run).astype(I32) for r in range(1, RUNS))
    table_ref[3] = jnp.where(total > 0, end, SLOTS)
    table_ref[4] = jnp.where((total > 0) & (last_run > first_run), last_run * run - 1, SLOTS)


def kernel(
    sol_ref, mean_ref, kl_ref, mi_ref, out_ref,
    vsol, vmean, vkl, vmi, send_v, send_k, modes, fields, zface, mean_blocks,
    halo_src_z, halo_src_x, halo_z, halo_x, diff, face, images, sums, result, table, table_s,
    load_sem, vs_sem, vr_sem, ks_sem, kr_sem, zs_sem, zr_sem, hs_sem, hr_sem, os_sem, or_sem, table_sem,
):
    s, c = lax.axis_index("space"), lax.axis_index("chaos")
    up, down = lax.rem(s + 1, SLABS), lax.rem(s + SLABS - 1, SLABS)
    block = block_of(s, c)
    up_c, down_c = chaos_of(up, block), chaos_of(down, block)
    next_c = chaos_of(s, lax.rem(block + 1, GROUPS))
    prev_c = chaos_of(s, lax.rem(block + GROUPS - 1, GROUPS))

    barrier = pltpu.get_barrier_semaphore()
    peers = [(s, lax.rem(c + d, GROUPS)) for d in range(1, GROUPS)]
    peers += [(up, c), (down, c), (up, up_c), (down, down_c)]
    for peer in peers:
        pl.semaphore_signal(barrier, inc=1, device_id=peer, device_id_type=MESH)

    loads = [
        pltpu.make_async_copy(src, dst, load_sem.at[i])
        for i, (src, dst) in enumerate(((sol_ref, vsol), (kl_ref, vkl), (mean_ref, vmean), (mi_ref, vmi)))
    ]
    for load in loads:
        load.start()

    loads[0].wait()

    @pl.loop(0, MODES, unroll=4)
    def _(i):
        for t in range(4):
            rows = pl.ds(8 * t, 8)
            low, high = halves(vsol[i, 0, rows, :], vsol[i, 1, rows, :])
            send_v[2 * t, i] = low
            send_v[2 * t + 1, i] = high

    low4 = sublane() < 4
    sub4 = lax.rem(sublane(), 4)
    below_ok = s > 0
    above_ok = s < SLABS - 1
    has_next = block < GROUPS - 1
    has_prev = block > 0
    last_lane = lane() == 127

    first_lane = lane() == 0

    def planes(ref, at):
        return [ref[at, q] for q in range(5)]

    def term(f, g):
        return (f[0] * g[0] + f[1] * g[1]) + (f[3] * g[3] + f[4] * g[4]), f[2] * g[2]

    def gather(level, flux):
        return level + (flux - jnp.where(first_lane, 0.0, pltpu.roll(flux, 1, 1)))

    def mode_copy(d):
        target = in_peer(c, d)
        return pltpu.make_async_remote_copy(
            send_v.at[block_of(s, target)],
            modes.at[pl.ds(c * MODES, MODES)],
            vs_sem.at[d],
            vr_sem.at[c],
            device_id=(s, target),
            device_id_type=MESH,
        )

    def field_copy(d):
        target = in_peer(c, d)
        return pltpu.make_async_remote_copy(
            send_k.at[block_of(s, target)],
            fields.at[c],
            ks_sem.at[d],
            kr_sem.at[c],
            device_id=(s, target),
            device_id_type=MESH,
        )

    z_copies = [
        pltpu.make_async_remote_copy(
            src, dst, zs_sem.at[i], zr_sem.at[i], device_id=(up, c), device_id_type=MESH
        )
        for i, (src, dst) in enumerate(
            ((vkl.at[:, 2, 1], zface.at[pl.ds(0, FIELDS)]), (vmean.at[2, 1], zface.at[FIELDS]))
        )
    ]

    def send_faces_up():
        loads[1].wait()
        loads[2].wait()
        for copy in z_copies:
            copy.start()

    def send_modes():
        for d in range(1, GROUPS):
            mode_copy(d).start()

    def own_modes():
        @pl.loop(0, MODES, unroll=True)
        def _(i):
            modes[c * MODES + i] = send_v[block, i]

    def pack_fields():
        @pl.loop(0, FIELDS * 3, unroll=4)
        def _(q):
            k, dim = lax.div(q, 3), lax.rem(q, 3)
            for t in range(4):
                rows = pl.ds(8 * t, 8)
                low, high = halves(vkl[k, dim, 0, rows, :], vkl[k, dim, 1, rows, :])
                send_k[2 * t, q] = low
                send_k[2 * t + 1, q] = high

        for b in range(GROUPS):
            for k in range(FIELDS):
                for layer in range(2):
                    at = pl.ds(2 * k + layer, 1)
                    if b == 0:
                        send_k[b, FIELDS * 3, at, :] = jnp.zeros((1, 128), F32)
                    else:
                        send_k[b, FIELDS * 3, at, :] = vkl[k, 0, layer, pl.ds(4 * b - 1, 1), :]

    def pack_faces_below():
        for copy in z_copies:
            copy.wait()
        for pair in range(2):
            for t in range(4):
                rows = pl.ds(8 * t, 8)
                low, high = halves(zface[2 * pair, rows, :], zface[2 * pair + 1, rows, :])
                send_k[2 * t, FIELDS * 3 + 1 + pair] = low
                send_k[2 * t + 1, FIELDS * 3 + 1 + pair] = high

    def send_fields():
        for d in range(1, GROUPS):
            field_copy(d).start()

    def own_fields():
        @pl.loop(0, KL_TILES, unroll=True)
        def _(q):
            fields[c, q] = send_k[block, q]

    def halo_copies(group):
        cells = pl.ds(group * (MODES // 2), MODES // 2)
        targets = ((up, up_c), (down, down_c), (s, next_c), (s, prev_c))
        copies = []
        for i, target in enumerate(targets):
            source, buffer = (halo_src_z, halo_z) if i < 2 else (halo_src_x, halo_x)
            part = cells if i < 2 else group
            copies.append(
                pltpu.make_async_remote_copy(
                    source.at[i % 2, part],
                    buffer.at[i % 2, part],
                    hs_sem.at[i, group],
                    hr_sem.at[i, group],
                    device_id=target,
                    device_id_type=MESH,
                )
            )
        return copies

    def arrival(d):
        return in_source(c, d)

    def forward(group):
        @pl.loop(0, MODES // 2, unroll=True)
        def _(i):
            at = group * (MODES // 2) + i
            low, high = halves(modes[2 * at], modes[2 * at + 1])
            halo_src_z[0, at] = high
            halo_src_z[1, at] = low

        copies = halo_copies(group)
        copies[0].start()
        copies[1].start()
        for layer in range(2):
            for i in range(MODES):
                m = group * MODES + i
                at = pl.ds(i, 1)
                halo_src_x[0, group, layer, at, :] = modes[m, pl.ds(4 * layer + 3, 1), :]
                halo_src_x[1, group, layer, at, :] = modes[m, pl.ds(4 * layer, 1), :]
        pl.when(has_next)(copies[2].start)
        pl.when(has_prev)(copies[3].start)

    def forward_arrivals(first, last):
        @pl.loop(first, last)
        def _(d):
            group = arrival(d)
            pltpu.make_async_copy(send_v.at[0], modes.at[pl.ds(group * MODES, MODES)], vr_sem.at[group]).wait()
            forward(group)

    to_scalars = pltpu.make_async_copy(table, table_s, table_sem)

    def tables():
        loads[3].wait()
        make_tables(vmi, table)
        to_scalars.start()

    def mean_faces():
        for t in range(4):
            rows = pl.ds(8 * t, 8)
            parts = [halves(vmean[dim, 0, rows, :], vmean[dim, 1, rows, :]) for dim in range(3)]
            under = zface[FIELDS, rows, :]
            for h in range(2):
                b = 2 * t + h
                fx, fy, fz = (part[h] for part in parts)
                prior = pltpu.roll(fx, 1, 0)
                if b == 0:
                    prior = jnp.where(sub4 == 0, 0.0, prior)
                else:
                    edges = [row(vmean[0, layer, pl.ds(4 * b - 1, 1), :]) for layer in range(2)]
                    prior = jnp.where(sub4 == 0, jnp.where(low4, edges[0], edges[1]), prior)
                lower = under if h == 0 else pltpu.roll(under, 4, 0)
                lower = jnp.where(below_ok, lower, 0.0)
                for q, value in enumerate((fx, prior, fy, fz, jnp.where(low4, lower, pltpu.roll(fz, 4, 0)))):
                    mean_blocks[b, q] = value

    def differences(d):
        group = arrival(d)
        copies = halo_copies(group)
        copies[0].wait_recv()
        copies[1].wait_recv()
        pl.when(has_prev)(copies[2].wait_recv)
        pl.when(has_next)(copies[3].wait_recv)

        @pl.loop(0, MODES // 2, unroll=True)
        def _(i):
            cell = group * (MODES // 2) + i
            under = halo_z[0, cell]
            over = jnp.where(above_ok, halo_z[1, cell], 0.0)
            for odd in range(2):
                m = 2 * cell + odd
                at = pl.ds(2 * i + odd, 1)
                v = modes[m]
                before = jnp.where(low4, row(halo_x[0, group, 0, at, :]), row(halo_x[0, group, 1, at, :]))
                before = jnp.where(has_prev, before, 0.0)
                after = jnp.where(low4, row(halo_x[1, group, 0, at, :]), row(halo_x[1, group, 1, at, :]))
                after = jnp.where(has_next, after, 0.0)
                next_x = jnp.where(sub4 == 3, after, pltpu.roll(v, 7, 0))
                prev_x = jnp.where(sub4 == 0, before, pltpu.roll(v, 1, 0))
                next_y = jnp.where(last_lane, 0.0, pltpu.roll(v, 127, 1))
                swapped = pltpu.roll(v, 4, 0)
                next_z = jnp.where(low4, swapped, over if odd else pltpu.roll(over, 4, 0))
                prev_z = jnp.where(low4, pltpu.roll(under, 4, 0) if odd else under, swapped)
                steps = [v - other for other in (next_x, prev_x, next_y, next_z, prev_z)]
                for q, value in enumerate(steps):
                    diff[m, q] = value
                result[m] = gather(*term(planes(mean_blocks, block), steps))

    def faces(group):
        for k in range(FIELDS):
            fx, fy, fz = (fields[group, 3 * k + dim] for dim in range(3))
            edges = [row(fields[group, FIELDS * 3, pl.ds(2 * k + layer, 1), :]) for layer in range(2)]
            prior = jnp.where(sub4 == 0, jnp.where(low4, edges[0], edges[1]), pltpu.roll(fx, 1, 0))
            under = fields[group, FIELDS * 3 + 1 + k // 2]
            under = under if k % 2 == 0 else pltpu.roll(under, 4, 0)
            lower = jnp.where(low4, jnp.where(below_ok, under, 0.0), pltpu.roll(fz, 4, 0))
            for q, value in enumerate((fx, prior, fy, fz, lower)):
                face[group * FIELDS + k, q] = value

    def arrived_faces(first, last):
        @pl.loop(first, last)
        def _(d):
            group = arrival(d)
            pltpu.make_async_copy(send_k.at[0], fields.at[group], kr_sem.at[group]).wait()
            faces(group)

    def all_differences(first, last):
        pl.loop(first, last)(differences)

    pl.semaphore_wait(barrier, len(peers))
    send_modes()
    own_modes()
    forward(c)
    send_faces_up()
    pack_fields()
    tables()
    forward_arrivals(1, GROUPS)
    pack_faces_below()
    send_fields()
    own_fields()
    mean_faces()
    faces(c)
    all_differences(0, GROUPS)
    arrived_faces(1, GROUPS)
    to_scalars.wait()

    def result_copy(target):
        return pltpu.make_async_remote_copy(
            result.at[pl.ds(target * MODES, MODES)],
            out_ref.at[block],
            os_sem.at[target],
            or_sem.at[block],
            device_id=(s, target),
            device_id_type=MESH,
        )

    def send_result(target):
        pl.when(target != c)(lambda: result_copy(target).start())
        own = pltpu.make_async_copy(result.at[pl.ds(target * MODES, MODES)], out_ref.at[block], or_sem.at[block])
        pl.when(target == c)(own.start)

    def variables(p):
        code = table_s[2, 0, p]
        return code >> 7, (code >> 2) & (UNITS - 1), (code & 3) == 2

    def image(p):
        a, b, double = variables(p)
        raised = jnp.where(double, F32(ROOT2), F32(1.0))
        own = planes(diff, p)
        at = 2 * (p - FIRST_PAIR)
        images[at] = raised * gather(*term(planes(face, b), own))
        images[at + 1] = raised * gather(*term(planes(face, a), own))

    def pair(p):
        a, b, double = variables(p)
        weight = jnp.where(double, F32(0.5 * ROOT2), F32(1.0))
        level_a, flux_a = term(planes(face, a), planes(diff, 1 + b))
        level_b, flux_b = term(planes(face, b), planes(diff, 1 + a))
        result[p] = result[p] + weight * gather(level_a + level_b, flux_a + flux_b)

    def pair_group(target):
        @pl.loop(0, MODES, unroll=True)
        def _(i):
            pair(target * MODES + i)

        send_result(target)

    high = lax.div(c, 4)
    early = (1 - high) * (4 + lax.rem(lax.rem(c, 4) + 2, 4)) + high * 3
    pair_group(early)

    pl.loop(FIRST_PAIR, TOTAL, unroll=IMAGE_UNROLL)(image)

    zero = jnp.zeros((8, 128), F32)
    sums[SLOTS] = zero
    run = SLOTS // RUNS

    @pl.loop(0, run, init_carry=((I32(-1), zero),) * RUNS, unroll=SLOT_UNROLL)
    def _(t, carry):
        now = []
        for r, (before, held) in enumerate(carry):
            at = t + r * run
            code = table_s[at >> 7, 0, at & (TOTAL - 1)]
            unit = code & (UNITS - 1)
            held = jnp.where(unit == before, held, 0.0) + images[code >> 5]
            sums[at] = held
            now.append((unit, held))
        return tuple(now)

    zeroth = planes(diff, 0)

    @pl.loop(0, UNITS, init_carry=(zero, zero), unroll=UNIT_UNROLL)
    def total(i, carry):
        field = planes(face, i)
        partial = sums[table_s[3, 0, i]] + sums[table_s[4, 0, i]]
        result[1 + i] = result[1 + i] + gather(*term(field, zeroth)) + partial
        level, flux = term(field, planes(diff, 1 + i))
        return carry[0] + level, carry[1] + flux

    result[0] = result[0] + gather(*total)

    pl.loop(FIRST_PAIR, FULL_GROUP * MODES, unroll=True)(pair)

    @pl.loop(1, GROUPS + 1)
    def _(d):
        target = out_peer(c, d)

        @pl.when((target >= FULL_GROUP) & (target != early))
        def _():
            pair_group(target)

        @pl.when(target < FULL_GROUP)
        def _():
            send_result(target)

    for b in range(GROUPS):
        pltpu.make_async_copy(result.at[pl.ds(0, MODES)], out_ref.at[b], or_sem.at[b]).wait()
    for d in range(1, GROUPS):
        mode_copy(d).wait_send()
        field_copy(d).wait_send()
        result_copy(peer_of(c, d)).wait_send()

    @pl.loop(0, GROUPS)
    def _(d):
        copies = halo_copies(arrival(d))
        copies[0].wait_send()
        copies[1].wait_send()
        pl.when(has_next)(copies[2].wait_send)
        pl.when(has_prev)(copies[3].wait_send)


def unpack(blocks_ref, out_ref, landed, final, in_sem, out_sem):
    loads, stores = [], []
    for t in range(4):
        part = pl.ds(2 * t, 2)
        loads.append(pltpu.make_async_copy(blocks_ref.at[part], landed.at[part], in_sem.at[t]))
        loads[-1].start()
    for t in range(4):
        rows = pl.ds(8 * t, 8)
        loads[t].wait()
        for i in range(MODES):
            low, high = halves(landed[2 * t, i], landed[2 * t + 1, i])
            final[i, 0, rows, :] = low
            final[i, 1, rows, :] = high
        stores.append(pltpu.make_async_copy(final.at[:, :, rows], out_ref.at[:, :, rows], out_sem.at[t]))
        stores[-1].start()
    for store in stores:
        store.wait()


def shards(sol, mean, kl, multi_index, couplings):
    tile = (8, 128)
    sem = pltpu.SemaphoreType.DMA
    blocks = pl.pallas_call(
        kernel,
        out_shape=jax.ShapeDtypeStruct((GROUPS, MODES) + tile, F32),
        in_specs=[pl.BlockSpec(memory_space=pltpu.HBM)] * 4,
        out_specs=pl.BlockSpec(memory_space=pl.ANY),
        scratch_shapes=[
            pltpu.VMEM((MODES, 2, 32, 128), F32),
            pltpu.VMEM((3, 2, 32, 128), F32),
            pltpu.VMEM((FIELDS, 3, 2, 32, 128), F32),
            pltpu.VMEM((UNITS, TOTAL), I32),
            pltpu.VMEM((GROUPS, MODES) + tile, F32),
            pltpu.VMEM((GROUPS, KL_TILES) + tile, F32),
            pltpu.VMEM((TOTAL,) + tile, F32),
            pltpu.VMEM((GROUPS, KL_TILES) + tile, F32),
            pltpu.VMEM((FIELDS + 1, 32, 128), F32),
            pltpu.VMEM((GROUPS, 5) + tile, F32),
            pltpu.VMEM((2, TOTAL // 2) + tile, F32),
            pltpu.VMEM((2, GROUPS, 2, MODES, 128), F32),
            pltpu.VMEM((2, TOTAL // 2) + tile, F32),
            pltpu.VMEM((2, GROUPS, 2, MODES, 128), F32),
            pltpu.VMEM((TOTAL, 5) + tile, F32),
            pltpu.VMEM((UNITS, 5) + tile, F32),
            pltpu.VMEM((SLOTS,) + tile, F32),
            pltpu.VMEM((SLOTS + 1,) + tile, F32),
            pltpu.VMEM((TOTAL,) + tile, F32),
            pltpu.VMEM((5,) + tile, I32),
            pltpu.SMEM((5,) + tile, I32),
            sem((4,)),
            sem((GROUPS,)),
            sem((GROUPS,)),
            sem((GROUPS,)),
            sem((GROUPS,)),
            sem((2,)),
            sem((2,)),
            sem((4, GROUPS)),
            sem((4, GROUPS)),
            sem((GROUPS,)),
            sem((GROUPS,)),
            sem,
        ],
        compiler_params=pltpu.CompilerParams(
            collective_id=0, has_side_effects=True, vmem_limit_bytes=60 * 2**20
        ),
        name="apply",
    )(sol, mean, kl, multi_index.T)
    return pl.pallas_call(
        unpack,
        out_shape=jax.ShapeDtypeStruct((MODES, 2, 32, 128), F32),
        in_specs=[pl.BlockSpec(memory_space=pl.ANY)],
        out_specs=pl.BlockSpec(memory_space=pl.ANY),
        scratch_shapes=[
            pltpu.VMEM((GROUPS, MODES) + tile, F32),
            pltpu.VMEM((MODES, 2, 32, 128), F32),
            sem((4,)),
            sem((4,)),
        ],
        compiler_params=pltpu.CompilerParams(vmem_limit_bytes=60 * 2**20),
        name="unpack",
    )(blocks)


def solution(mesh):
    return jax.shard_map(
        shards,
        mesh=mesh,
        in_specs=(
            P("chaos", "space", None, None),
            P(None, "space", None, None),
            P("chaos", None, "space", None, None),
            P(),
            P(),
        ),
        out_specs=P("chaos", "space", None, None),
        check_vma=False,
    )
```

```python
import math

import jax
import jax.numpy as jnp
from jax import lax
from jax.experimental import pallas as pl
from jax.experimental.pallas import tpu as pltpu
from jax.sharding import PartitionSpec as P

MESH = pl.DeviceIdType.MESH
F32 = jnp.float32
I32 = jnp.int32
SLABS = 16
GROUPS = 8
MODES = 16
FIELDS = 4
KL_TILES = FIELDS * 3 + 3
UNITS = 32
FIRST_PAIR = 33
TOTAL = 128
SLOTS = 192
FULL_GROUP = 3
IMAGE_UNROLL = 95
SLOT_UNROLL = 48
RUNS = 4
UNIT_UNROLL = 32
ROOT2 = math.sqrt(2.0)


def flip_of(slab):
    return lax.rem(lax.div(slab, 4), 2)


def block_of(slab, chaos):
    high = lax.rem(lax.div(chaos, 4) + flip_of(slab), 2)
    y = lax.rem(lax.rem(chaos, 4) + 1, 4)
    return high * 4 + high * (3 - y) + (1 - high) * y


def chaos_of(slab, block):
    high = lax.div(block, 4)
    low = lax.rem(block, 4)
    y = lax.rem(high * (3 - low) + (1 - high) * low + 3, 4)
    return lax.rem(high + flip_of(slab), 2) * 4 + y


def peer_of(chaos, d):
    high = lax.rem(lax.div(chaos, 4) + lax.div(d, 4), 2)
    return high * 4 + lax.rem(lax.rem(chaos, 4) + lax.rem(d, 4), 4)


def source_of(chaos, d):
    high = lax.rem(lax.div(chaos, 4) + lax.div(d, 4), 2)
    return high * 4 + lax.rem(lax.rem(chaos, 4) + 4 - lax.rem(d, 4), 4)


def out_peer(chaos, d):
    d = lax.rem(d, 8)
    move = d * 0
    move = move + jnp.where(d == 1, 6, 0)
    move = move + jnp.where(d == 2, 2, 0)
    move = move + jnp.where(d == 3, 5, 0)
    move = move + jnp.where(d == 4, 7, 0)
    move = move + jnp.where(d == 5, 4, 0)
    move = move + jnp.where(d == 6, 1, 0)
    move = move + jnp.where(d == 7, 3, 0)
    high = lax.rem(lax.div(chaos, 4) + lax.div(move, 4), 2)
    return high * 4 + lax.rem(lax.rem(chaos, 4) + lax.rem(move, 4), 4)


def field_peer(chaos, d):
    d = lax.rem(d, 8)
    move = d * 0
    move = move + jnp.where(d == 1, 2, 0)
    move = move + jnp.where(d == 2, 6, 0)
    move = move + jnp.where(d == 3, 1, 0)
    move = move + jnp.where(d == 4, 5, 0)
    move = move + jnp.where(d == 5, 3, 0)
    move = move + jnp.where(d == 6, 7, 0)
    move = move + jnp.where(d == 7, 4, 0)
    high = lax.rem(lax.div(chaos, 4) + lax.div(move, 4), 2)
    return high * 4 + lax.rem(lax.rem(chaos, 4) + lax.rem(move, 4), 4)


def in_peer(chaos, d):
    d = lax.rem(d, 8)
    move = d * 0
    move = move + jnp.where(d == 1, 6, 0)
    move = move + jnp.where(d == 2, 2, 0)
    move = move + jnp.where(d == 3, 5, 0)
    move = move + jnp.where(d == 4, 7, 0)
    move = move + jnp.where(d == 5, 4, 0)
    move = move + jnp.where(d == 6, 1, 0)
    move = move + jnp.where(d == 7, 3, 0)
    high = lax.rem(lax.div(chaos, 4) + lax.div(move, 4), 2)
    return high * 4 + lax.rem(lax.rem(chaos, 4) + lax.rem(move, 4), 4)


def in_source(chaos, d):
    d = lax.rem(d, 8)
    move = d * 0
    move = move + jnp.where(d == 1, 6, 0)
    move = move + jnp.where(d == 2, 2, 0)
    move = move + jnp.where(d == 3, 5, 0)
    move = move + jnp.where(d == 4, 7, 0)
    move = move + jnp.where(d == 5, 4, 0)
    move = move + jnp.where(d == 6, 1, 0)
    move = move + jnp.where(d == 7, 3, 0)
    high = lax.rem(lax.div(chaos, 4) + lax.div(move, 4), 2)
    return high * 4 + lax.rem(lax.rem(chaos, 4) + 4 - lax.rem(move, 4), 4)


def sublane():
    return lax.broadcasted_iota(I32, (8, 128), 0)


def lane():
    return lax.broadcasted_iota(I32, (8, 128), 1)


def halves(a, b):
    low = sublane() < 4
    return jnp.where(low, a, pltpu.roll(b, 4, 0)), jnp.where(low, pltpu.roll(a, 4, 0), b)


def row(ref_row):
    return jnp.broadcast_to(ref_row, (8, 128))


def make_tables(mi_ref, table_ref):
    shape = (TOTAL, TOTAL)
    mode = lax.broadcasted_iota(I32, shape, 0)
    var = lax.broadcasted_iota(I32, shape, 1)
    degree = jnp.concatenate([mi_ref[...], jnp.zeros((TOTAL - UNITS, TOTAL), I32)], axis=0).T
    is_pair = mode >= FIRST_PAIR
    held = (degree > 0) & is_pair
    count = held.astype(I32)
    running = count
    step = 1
    while step < TOTAL:
        running = running + jnp.where(mode >= step, pltpu.roll(running, step, 0), 0)
        step *= 2
    total = jnp.broadcast_to(running[TOTAL - 1 :, :], (8, TOTAL))
    var8 = lax.broadcasted_iota(I32, (8, TOTAL), 1)
    prefix = total
    step = 1
    while step < UNITS:
        prefix = prefix + jnp.where(var8 >= step, pltpu.roll(prefix, step, 1), 0)
        step *= 2
    start = prefix - total
    place = running - count + jnp.broadcast_to(start[:1, :], shape)
    first = jnp.min(jnp.where(held, var, TOTAL), axis=1, keepdims=True)
    last = jnp.max(jnp.where(held, var, -1), axis=1, keepdims=True)
    place_a = jnp.max(jnp.where(held & (var == first), place, -1), axis=1, keepdims=True)
    place_b = jnp.max(jnp.where(held & (var == last), place, -1), axis=1, keepdims=True)
    column = lax.broadcasted_iota(I32, (TOTAL, 1), 0)
    pair = column >= FIRST_PAIR
    double = first == last
    kind = jnp.where(double, 2, 1)
    first = jnp.where(pair, jnp.minimum(first, UNITS - 1), 0)
    last = jnp.where(pair, jnp.maximum(last, 0), 0)
    code_a = jnp.where(pair, (column - FIRST_PAIR) * 2 * UNITS + first, 0)
    code_b = jnp.where(pair & jnp.logical_not(double), ((column - FIRST_PAIR) * 2 + 1) * UNITS + last, 0)
    code_p = (first * UNITS + last) * 4 + kind
    for half in range(2):
        slot = var + half * TOTAL
        code = jnp.where(place_a == slot, code_a, 0) + jnp.where(place_b == slot, code_b, 0)
        table_ref[half] = jnp.broadcast_to(jnp.sum(code, axis=0, keepdims=True), (8, TOTAL))
    table_ref[2] = jnp.broadcast_to(
        jnp.sum(jnp.where(mode == var, code_p, 0), axis=0, keepdims=True), (8, TOTAL)
    )
    end = prefix - 1
    run = SLOTS // RUNS
    first_run = sum((start >= r * run).astype(I32) for r in range(1, RUNS))
    last_run = sum((end >= r * run).astype(I32) for r in range(1, RUNS))
    table_ref[3] = jnp.where(total > 0, end, SLOTS)
    table_ref[4] = jnp.where((total > 0) & (last_run > first_run), last_run * run - 1, SLOTS)


def kernel(
    sol_ref, mean_ref, kl_ref, mi_ref, out_ref,
    vsol, vmean, vkl, vmi, send_v, send_k, modes, fields, zface, mean_blocks,
    halo_src_z, halo_src_x, halo_z, halo_x, diff, face, images, sums, result, table, table_s,
    load_sem, vs_sem, vr_sem, ks_sem, kr_sem, zs_sem, zr_sem, hs_sem, hr_sem, os_sem, or_sem, table_sem,
):
    s, c = lax.axis_index("space"), lax.axis_index("chaos")
    up, down = lax.rem(s + 1, SLABS), lax.rem(s + SLABS - 1, SLABS)
    block = block_of(s, c)
    up_c, down_c = chaos_of(up, block), chaos_of(down, block)
    next_c = chaos_of(s, lax.rem(block + 1, GROUPS))
    prev_c = chaos_of(s, lax.rem(block + GROUPS - 1, GROUPS))

    barrier = pltpu.get_barrier_semaphore()
    peers = [(s, lax.rem(c + d, GROUPS)) for d in range(1, GROUPS)]
    peers += [(up, c), (down, c), (up, up_c), (down, down_c)]
    for peer in peers:
        pl.semaphore_signal(barrier, inc=1, device_id=peer, device_id_type=MESH)

    loads = [
        pltpu.make_async_copy(src, dst, load_sem.at[i])
        for i, (src, dst) in enumerate(((sol_ref, vsol), (kl_ref, vkl), (mean_ref, vmean), (mi_ref, vmi)))
    ]
    for load in loads:
        load.start()

    loads[0].wait()

    @pl.loop(0, MODES, unroll=4)
    def _(i):
        for t in range(4):
            rows = pl.ds(8 * t, 8)
            low, high = halves(vsol[i, 0, rows, :], vsol[i, 1, rows, :])
            send_v[2 * t, i] = low
            send_v[2 * t + 1, i] = high

    low4 = sublane() < 4
    sub4 = lax.rem(sublane(), 4)
    below_ok = s > 0
    above_ok = s < SLABS - 1
    has_next = block < GROUPS - 1
    has_prev = block > 0
    last_lane = lane() == 127

    first_lane = lane() == 0

    def planes(ref, at):
        return [ref[at, q] for q in range(5)]

    def term(f, g):
        return (f[0] * g[0] + f[1] * g[1]) + (f[3] * g[3] + f[4] * g[4]), f[2] * g[2]

    def gather(level, flux):
        return level + (flux - jnp.where(first_lane, 0.0, pltpu.roll(flux, 1, 1)))

    def mode_copy(d):
        target = in_peer(c, d)
        return pltpu.make_async_remote_copy(
            send_v.at[block_of(s, target)],
            modes.at[pl.ds(c * MODES, MODES)],
            vs_sem.at[d],
            vr_sem.at[c],
            device_id=(s, target),
            device_id_type=MESH,
        )

    def field_copy(d):
        target = field_peer(c, d)
        return pltpu.make_async_remote_copy(
            send_k.at[block_of(s, target)],
            fields.at[c],
            ks_sem.at[d],
            kr_sem.at[c],
            device_id=(s, target),
            device_id_type=MESH,
        )

    z_copies = [
        pltpu.make_async_remote_copy(
            src, dst, zs_sem.at[i], zr_sem.at[i], device_id=(up, c), device_id_type=MESH
        )
        for i, (src, dst) in enumerate(
            ((vkl.at[:, 2, 1], zface.at[pl.ds(0, FIELDS)]), (vmean.at[2, 1], zface.at[FIELDS]))
        )
    ]

    def send_faces_up():
        loads[1].wait()
        loads[2].wait()
        for copy in z_copies:
            copy.start()

    def send_modes():
        for d in range(1, GROUPS):
            mode_copy(d).start()

    def own_modes():
        @pl.loop(0, MODES, unroll=True)
        def _(i):
            modes[c * MODES + i] = send_v[block, i]

    def pack_fields():
        @pl.loop(0, FIELDS * 3, unroll=4)
        def _(q):
            k, dim = lax.div(q, 3), lax.rem(q, 3)
            for t in range(4):
                rows = pl.ds(8 * t, 8)
                low, high = halves(vkl[k, dim, 0, rows, :], vkl[k, dim, 1, rows, :])
                send_k[2 * t, q] = low
                send_k[2 * t + 1, q] = high

        for b in range(GROUPS):
            for k in range(FIELDS):
                for layer in range(2):
                    at = pl.ds(2 * k + layer, 1)
                    if b == 0:
                        send_k[b, FIELDS * 3, at, :] = jnp.zeros((1, 128), F32)
                    else:
                        send_k[b, FIELDS * 3, at, :] = vkl[k, 0, layer, pl.ds(4 * b - 1, 1), :]

    def pack_faces_below():
        for copy in z_copies:
            copy.wait()
        for pair in range(2):
            for t in range(4):
                rows = pl.ds(8 * t, 8)
                low, high = halves(zface[2 * pair, rows, :], zface[2 * pair + 1, rows, :])
                send_k[2 * t, FIELDS * 3 + 1 + pair] = low
                send_k[2 * t + 1, FIELDS * 3 + 1 + pair] = high

    def send_fields():
        for d in range(1, GROUPS):
            field_copy(d).start()

    def own_fields():
        @pl.loop(0, KL_TILES, unroll=True)
        def _(q):
            fields[c, q] = send_k[block, q]

    def halo_copies(group):
        cells = pl.ds(group * (MODES // 2), MODES // 2)
        targets = ((up, up_c), (down, down_c), (s, next_c), (s, prev_c))
        copies = []
        for i, target in enumerate(targets):
            source, buffer = (halo_src_z, halo_z) if i < 2 else (halo_src_x, halo_x)
            part = cells if i < 2 else group
            copies.append(
                pltpu.make_async_remote_copy(
                    source.at[i % 2, part],
                    buffer.at[i % 2, part],
                    hs_sem.at[i, group],
                    hr_sem.at[i, group],
                    device_id=target,
                    device_id_type=MESH,
                )
            )
        return copies

    def arrival(d):
        return in_source(c, d)

    def forward(group):
        @pl.loop(0, MODES // 2, unroll=True)
        def _(i):
            at = group * (MODES // 2) + i
            low, high = halves(modes[2 * at], modes[2 * at + 1])
            halo_src_z[0, at] = high
            halo_src_z[1, at] = low

        copies = halo_copies(group)
        copies[0].start()
        copies[1].start()
        for layer in range(2):
            for i in range(MODES):
                m = group * MODES + i
                at = pl.ds(i, 1)
                halo_src_x[0, group, layer, at, :] = modes[m, pl.ds(4 * layer + 3, 1), :]
                halo_src_x[1, group, layer, at, :] = modes[m, pl.ds(4 * layer, 1), :]
        pl.when(has_next)(copies[2].start)
        pl.when(has_prev)(copies[3].start)

    def forward_arrivals(first, last):
        @pl.loop(first, last)
        def _(d):
            group = arrival(d)
            pltpu.make_async_copy(send_v.at[0], modes.at[pl.ds(group * MODES, MODES)], vr_sem.at[group]).wait()
            forward(group)

    to_scalars = pltpu.make_async_copy(table, table_s, table_sem)

    def tables():
        loads[3].wait()
        make_tables(vmi, table)
        to_scalars.start()

    def mean_faces():
        for t in range(4):
            rows = pl.ds(8 * t, 8)
            parts = [halves(vmean[dim, 0, rows, :], vmean[dim, 1, rows, :]) for dim in range(3)]
            under = zface[FIELDS, rows, :]
            for h in range(2):
                b = 2 * t + h
                fx, fy, fz = (part[h] for part in parts)
                prior = pltpu.roll(fx, 1, 0)
                if b == 0:
                    prior = jnp.where(sub4 == 0, 0.0, prior)
                else:
                    edges = [row(vmean[0, layer, pl.ds(4 * b - 1, 1), :]) for layer in range(2)]
                    prior = jnp.where(sub4 == 0, jnp.where(low4, edges[0], edges[1]), prior)
                lower = under if h == 0 else pltpu.roll(under, 4, 0)
                lower = jnp.where(below_ok, lower, 0.0)
                for q, value in enumerate((fx, prior, fy, fz, jnp.where(low4, lower, pltpu.roll(fz, 4, 0)))):
                    mean_blocks[b, q] = value

    def differences(d):
        group = arrival(d)
        copies = halo_copies(group)
        copies[0].wait_recv()
        copies[1].wait_recv()
        pl.when(has_prev)(copies[2].wait_recv)
        pl.when(has_next)(copies[3].wait_recv)

        @pl.loop(0, MODES // 2, unroll=True)
        def _(i):
            cell = group * (MODES // 2) + i
            under = halo_z[0, cell]
            over = jnp.where(above_ok, halo_z[1, cell], 0.0)
            for odd in range(2):
                m = 2 * cell + odd
                at = pl.ds(2 * i + odd, 1)
                v = modes[m]
                before = jnp.where(low4, row(halo_x[0, group, 0, at, :]), row(halo_x[0, group, 1, at, :]))
                before = jnp.where(has_prev, before, 0.0)
                after = jnp.where(low4, row(halo_x[1, group, 0, at, :]), row(halo_x[1, group, 1, at, :]))
                after = jnp.where(has_next, after, 0.0)
                next_x = jnp.where(sub4 == 3, after, pltpu.roll(v, 7, 0))
                prev_x = jnp.where(sub4 == 0, before, pltpu.roll(v, 1, 0))
                next_y = jnp.where(last_lane, 0.0, pltpu.roll(v, 127, 1))
                swapped = pltpu.roll(v, 4, 0)
                next_z = jnp.where(low4, swapped, over if odd else pltpu.roll(over, 4, 0))
                prev_z = jnp.where(low4, pltpu.roll(under, 4, 0) if odd else under, swapped)
                steps = [v - other for other in (next_x, prev_x, next_y, next_z, prev_z)]
                for q, value in enumerate(steps):
                    diff[m, q] = value
                result[m] = gather(*term(planes(mean_blocks, block), steps))

    def faces(group):
        for k in range(FIELDS):
            fx, fy, fz = (fields[group, 3 * k + dim] for dim in range(3))
            edges = [row(fields[group, FIELDS * 3, pl.ds(2 * k + layer, 1), :]) for layer in range(2)]
            prior = jnp.where(sub4 == 0, jnp.where(low4, edges[0], edges[1]), pltpu.roll(fx, 1, 0))
            under = fields[group, FIELDS * 3 + 1 + k // 2]
            under = under if k % 2 == 0 else pltpu.roll(under, 4, 0)
            lower = jnp.where(low4, jnp.where(below_ok, under, 0.0), pltpu.roll(fz, 4, 0))
            for q, value in enumerate((fx, prior, fy, fz, lower)):
                face[group * FIELDS + k, q] = value

    def arrived_faces(first, last):
        @pl.loop(first, last)
        def _(d):
            group = arrival(d)
            pltpu.make_async_copy(send_k.at[0], fields.at[group], kr_sem.at[group]).wait()
            faces(group)

    def all_differences(first, last):
        pl.loop(first, last)(differences)

    pl.semaphore_wait(barrier, len(peers))
    send_modes()
    own_modes()
    forward(c)
    send_faces_up()
    pack_fields()
    tables()
    forward_arrivals(1, GROUPS)
    pack_faces_below()
    send_fields()
    mean_faces()
    own_fields()
    faces(c)
    all_differences(0, GROUPS)
    arrived_faces(1, GROUPS)
    to_scalars.wait()

    def result_copy(target):
        return pltpu.make_async_remote_copy(
            result.at[pl.ds(target * MODES, MODES)],
            out_ref.at[block],
            os_sem.at[target],
            or_sem.at[block],
            device_id=(s, target),
            device_id_type=MESH,
        )

    def send_result(target):
        pl.when(target != c)(lambda: result_copy(target).start())
        own = pltpu.make_async_copy(result.at[pl.ds(target * MODES, MODES)], out_ref.at[block], or_sem.at[block])
        pl.when(target == c)(own.start)

    def variables(p):
        code = table_s[2, 0, p]
        return code >> 7, (code >> 2) & (UNITS - 1), (code & 3) == 2

    def image(p):
        a, b, double = variables(p)
        raised = jnp.where(double, F32(ROOT2), F32(1.0))
        own = planes(diff, p)
        at = 2 * (p - FIRST_PAIR)
        images[at] = raised * gather(*term(planes(face, b), own))
        images[at + 1] = raised * gather(*term(planes(face, a), own))

    def pair(p):
        a, b, double = variables(p)
        weight = jnp.where(double, F32(0.5 * ROOT2), F32(1.0))
        level_a, flux_a = term(planes(face, a), planes(diff, 1 + b))
        level_b, flux_b = term(planes(face, b), planes(diff, 1 + a))
        result[p] = result[p] + weight * gather(level_a + level_b, flux_a + flux_b)

    def pair_group(target):
        @pl.loop(0, MODES, unroll=True)
        def _(i):
            pair(target * MODES + i)

        send_result(target)

    high = lax.div(c, 4)
    early = (1 - high) * (4 + lax.rem(lax.rem(c, 4) + 2, 4)) + high * 3
    pair_group(early)

    pl.loop(FIRST_PAIR, TOTAL, unroll=IMAGE_UNROLL)(image)

    zero = jnp.zeros((8, 128), F32)
    sums[SLOTS] = zero
    run = SLOTS // RUNS

    @pl.loop(0, run, init_carry=((I32(-1), zero),) * RUNS, unroll=SLOT_UNROLL)
    def _(t, carry):
        now = []
        for r, (before, held) in enumerate(carry):
            at = t + r * run
            code = table_s[at >> 7, 0, at & (TOTAL - 1)]
            unit = code & (UNITS - 1)
            held = jnp.where(unit == before, held, 0.0) + images[code >> 5]
            sums[at] = held
            now.append((unit, held))
        return tuple(now)

    zeroth = planes(diff, 0)

    @pl.loop(0, UNITS, init_carry=(zero, zero), unroll=UNIT_UNROLL)
    def total(i, carry):
        field = planes(face, i)
        partial = sums[table_s[3, 0, i]] + sums[table_s[4, 0, i]]
        result[1 + i] = result[1 + i] + gather(*term(field, zeroth)) + partial
        level, flux = term(field, planes(diff, 1 + i))
        return carry[0] + level, carry[1] + flux

    result[0] = result[0] + gather(*total)

    pl.loop(FIRST_PAIR, FULL_GROUP * MODES, unroll=True)(pair)

    @pl.loop(1, GROUPS + 1)
    def _(d):
        target = out_peer(c, d)

        @pl.when((target >= FULL_GROUP) & (target != early))
        def _():
            pair_group(target)

        @pl.when(target < FULL_GROUP)
        def _():
            send_result(target)

    for b in range(GROUPS):
        pltpu.make_async_copy(result.at[pl.ds(0, MODES)], out_ref.at[b], or_sem.at[b]).wait()
    for d in range(1, GROUPS):
        mode_copy(d).wait_send()
        field_copy(d).wait_send()
        result_copy(peer_of(c, d)).wait_send()

    @pl.loop(0, GROUPS)
    def _(d):
        copies = halo_copies(arrival(d))
        copies[0].wait_send()
        copies[1].wait_send()
        pl.when(has_next)(copies[2].wait_send)
        pl.when(has_prev)(copies[3].wait_send)


def unpack(blocks_ref, out_ref, landed, final, in_sem, out_sem):
    loads, stores = [], []
    for t in range(4):
        part = pl.ds(2 * t, 2)
        loads.append(pltpu.make_async_copy(blocks_ref.at[part], landed.at[part], in_sem.at[t]))
        loads[-1].start()
    for t in range(4):
        rows = pl.ds(8 * t, 8)
        loads[t].wait()
        for i in range(MODES):
            low, high = halves(landed[2 * t, i], landed[2 * t + 1, i])
            final[i, 0, rows, :] = low
            final[i, 1, rows, :] = high
        stores.append(pltpu.make_async_copy(final.at[:, :, rows], out_ref.at[:, :, rows], out_sem.at[t]))
        stores[-1].start()
    for store in stores:
        store.wait()


def shards(sol, mean, kl, multi_index, couplings):
    tile = (8, 128)
    sem = pltpu.SemaphoreType.DMA
    blocks = pl.pallas_call(
        kernel,
        out_shape=jax.ShapeDtypeStruct((GROUPS, MODES) + tile, F32),
        in_specs=[pl.BlockSpec(memory_space=pltpu.HBM)] * 4,
        out_specs=pl.BlockSpec(memory_space=pl.ANY),
        scratch_shapes=[
            pltpu.VMEM((MODES, 2, 32, 128), F32),
            pltpu.VMEM((3, 2, 32, 128), F32),
            pltpu.VMEM((FIELDS, 3, 2, 32, 128), F32),
            pltpu.VMEM((UNITS, TOTAL), I32),
            pltpu.VMEM((GROUPS, MODES) + tile, F32),
            pltpu.VMEM((GROUPS, KL_TILES) + tile, F32),
            pltpu.VMEM((TOTAL,) + tile, F32),
            pltpu.VMEM((GROUPS, KL_TILES) + tile, F32),
            pltpu.VMEM((FIELDS + 1, 32, 128), F32),
            pltpu.VMEM((GROUPS, 5) + tile, F32),
            pltpu.VMEM((2, TOTAL // 2) + tile, F32),
            pltpu.VMEM((2, GROUPS, 2, MODES, 128), F32),
            pltpu.VMEM((2, TOTAL // 2) + tile, F32),
            pltpu.VMEM((2, GROUPS, 2, MODES, 128), F32),
            pltpu.VMEM((TOTAL, 5) + tile, F32),
            pltpu.VMEM((UNITS, 5) + tile, F32),
            pltpu.VMEM((SLOTS,) + tile, F32),
            pltpu.VMEM((SLOTS + 1,) + tile, F32),
            pltpu.VMEM((TOTAL,) + tile, F32),
            pltpu.VMEM((5,) + tile, I32),
            pltpu.SMEM((5,) + tile, I32),
            sem((4,)),
            sem((GROUPS,)),
            sem((GROUPS,)),
            sem((GROUPS,)),
            sem((GROUPS,)),
            sem((2,)),
            sem((2,)),
            sem((4, GROUPS)),
            sem((4, GROUPS)),
            sem((GROUPS,)),
            sem((GROUPS,)),
            sem,
        ],
        compiler_params=pltpu.CompilerParams(
            collective_id=0, has_side_effects=True, vmem_limit_bytes=60 * 2**20
        ),
        name="apply",
    )(sol, mean, kl, multi_index.T)
    return pl.pallas_call(
        unpack,
        out_shape=jax.ShapeDtypeStruct((MODES, 2, 32, 128), F32),
        in_specs=[pl.BlockSpec(memory_space=pl.ANY)],
        out_specs=pl.BlockSpec(memory_space=pl.ANY),
        scratch_shapes=[
            pltpu.VMEM((GROUPS, MODES) + tile, F32),
            pltpu.VMEM((MODES, 2, 32, 128), F32),
            sem((4,)),
            sem((4,)),
        ],
        compiler_params=pltpu.CompilerParams(vmem_limit_bytes=60 * 2**20),
        name="unpack",
    )(blocks)


def solution(mesh):
    return jax.shard_map(
        shards,
        mesh=mesh,
        in_specs=(
            P("chaos", "space", None, None),
            P(None, "space", None, None),
            P("chaos", None, "space", None, None),
            P(),
            P(),
        ),
        out_specs=P("chaos", "space", None, None),
        check_vma=False,
    )
```
